32 devices in a mesh: dp: 4 (over y, x), expert: 8 (over z, core).
Axes of the slice: x: 2, y: 2, z: 4, core: 2. Of those that a mesh axis runs over, the one named last changes fastest.
Arguments:
- tokens: bfloat16 [256, 2048], P('dp'), may hold values from -6 to 6
- d_mixed: bfloat16 [256, 2048], P('dp'), may hold values from -6 to 6
- route_ids: int32 [256, 6], replicated, may hold values from 0 to 15, all different within a row; in each aligned block of 64 rows (0 to 63, 64 to 127, ...) at most 64 rows name the same one
- route_weight: float32 [256, 6], replicated, may hold values from 0.05 to 1
- gate_weight: bfloat16 [32, 704, 2048], P(('expert', 'dp')), may hold values from -0.125 to 0.125
- up_weight: bfloat16 [32, 704, 2048], P(('expert', 'dp')), may hold values from -0.125 to 0.125
- down_weight: bfloat16 [32, 704, 2048], P(('expert', 'dp')), may hold values from -0.15625 to 0.15625
Outputs:
- mixed: bfloat16 [256, 2048], P('dp')
- d_route: float32 [256, 6], P('dp')
- d_tokens: bfloat16 [256, 2048], P('dp')
- grad_gate: bfloat16 [32, 704, 2048], P(('expert', 'dp'))
- grad_up: bfloat16 [32, 704, 2048], P(('expert', 'dp'))
- grad_down: bfloat16 [32, 704, 2048], P(('expert', 'dp'))
The draws below stay inside these ranges and needn't reach their ends.
Inputs may be any that keep to these rules, and one draw needn't show every extreme that they name: `route_ids`: each row names 6 different experts. In each aligned block of 64 rows (the tokens of one index of dp) no expert is named by more than 64 rows, and in every draw some expert is named by exactly 64 rows of some block.
All inputs are finite; a program needn't handle non-finite values.
Results may differ from the reference program's by a relative error of at most 0.0064.
Values may be sent and summed in bfloat16 or wider, within the bound.
A program may use at most 64 MiB of HBM per device.

```python
import math
import jax
import jax.numpy as jnp
import numpy as np
from jax import lax

D = 2048
FF = 1408
TOP = 6
TOK_DEV = 64
EXPERTS = 16
PIECES = 2
HID = 704
TOKENS = 256
CAP = 64
N_DP = 4


def block_scale(stream_key, extent, cuts, low, high):
    def one(dim, shards_of):
        draws = jax.random.uniform(jax.random.fold_in(jax.random.fold_in(stream_key, 6), dim), (shards_of,), jnp.float32, low / len(cuts), high / len(cuts))
        return jnp.repeat(jnp.exp(draws), extent[dim] // shards_of).reshape((-1,) + (1,) * (len(extent) - dim - 1))

    gain = one(*cuts[0])
    for cut in cuts[1:]:
        gain = gain * one(*cut)
    return gain


def routed_block(key, own, number, rows, amount, top, reach, slope):
    sequence = jax.random.permutation(key, amount)
    heavy_load, common = portions_of(amount, rows * top, reach, slope, True), portions_of(amount, rows * top, reach, slope, False)
    places = jnp.arange(amount)

    def named(tallies, rotation):
        used = int((tallies > 0).sum())
        fixed = max(1, used // 4)
        passed = fixed + (places - fixed + rotation * (used - fixed)) % max(1, amount - fixed)
        return jnp.zeros((amount,), jnp.int32).at[sequence[jnp.where(places < fixed, places, passed)]].set(jnp.asarray(tallies, jnp.int32))

    tallies = jnp.where(number % 4 == 0, named(heavy_load, number // 4), named(common, number - number // 4 - 1))
    mixed = jax.random.permutation(jax.random.fold_in(own, 3), amount)
    donor, receiver = mixed[0:amount // 2 * 2:2], mixed[1:amount // 2 * 2:2]
    slack = jnp.minimum(tallies[donor] - 1, reach - tallies[receiver]) // 2
    slack = jnp.where((donor == sequence[0]) | (receiver == sequence[0]) | (tallies[receiver] == 0), 0, jnp.maximum(slack, 0))
    passed = jax.random.randint(jax.random.fold_in(own, 4), (amount // 2,), 0, 1 << 20) % (slack + 1)
    tallies = tallies.at[donor].add(-passed).at[receiver].add(passed)
    members = jnp.searchsorted(jnp.cumsum(tallies), jnp.arange(rows * top), side="right").astype(jnp.int32)
    listing = members.reshape(top, rows).T
    listing = listing[jax.random.permutation(jax.random.fold_in(own, 1), rows)]
    rotation = jax.random.randint(jax.random.fold_in(own, 2), (rows, 1), 0, top)
    return jnp.take_along_axis(listing, (jnp.arange(top)[None, :] + rotation) % top, axis=1)


def portions_of(amount, total, reach, skew, full):
    portions = [(1 << 20) // math.isqrt(grade ** skew) + 1 for grade in range(1, amount + 1)]
    largest = reach if full else min(reach, max(-(-total // amount), total * portions[0] // sum(portions)))
    least = 1 if total - largest >= amount - 1 else 0
    holding, rest = [largest] + [least] * (amount - 1), total - largest - least * (amount - 1)
    while rest > 0:
        candidates = [i for i in range(1, amount) if holding[i] < largest] or [i for i in range(1, amount) if holding[i] < reach]
        pool, remaining = sum([portions[i] for i in candidates]), rest
        for i in candidates:
            addition = min(reach - holding[i], max(1, remaining * portions[i] // pool), rest)
            holding[i] = holding[i] + addition
            rest = rest - addition
    return np.array(holding)


def bell_draw(key, dims, width, bound, pieces=(), kind=jnp.bfloat16):
    factor_of = block_scale(key, dims, pieces, -0.22, 0.18) if pieces else 1.0
    entries = jax.random.normal(key, dims, jnp.float32) * width * factor_of
    return jnp.minimum(jnp.maximum(entries, -bound), bound).astype(kind)


def setup_inputs(seed: int = 0) -> dict:
    seeds = jax.random.split(jax.random.key(seed), 8)
    tokens = bell_draw(seeds[0], (TOKENS, D), 1.0, 6.0, ((0, 4),))
    d_mixed = bell_draw(seeds[1], (TOKENS, D), 1.0, 6.0, ((0, 4),))
    route_ids_keys = jax.random.split(jax.random.fold_in(seeds[2], 1), TOKENS // TOK_DEV)
    route_ids_turns = jax.random.permutation(jax.random.fold_in(seeds[2], 3), TOKENS // TOK_DEV)
    route_ids = jax.vmap(lambda own, number: routed_block(jax.random.fold_in(seeds[2], 2), own, number, TOK_DEV, EXPERTS, TOP, CAP, 2))(route_ids_keys, route_ids_turns).reshape((TOKENS, TOP))
    route_weight = jnp.clip(jax.random.uniform(seeds[3], (TOKENS, TOP), jnp.float32, 0.05, 1.0), 0.05, 1.0)
    gate_weight = bell_draw(seeds[4], (EXPERTS * PIECES, HID, D), D ** -0.5, 0.125, ((0, 32),))
    up_weight = bell_draw(seeds[5], (EXPERTS * PIECES, HID, D), D ** -0.5, 0.125, ((0, 32),))
    down_weight = bell_draw(seeds[6], (EXPERTS * PIECES, HID, D), FF ** -0.5, 0.15625, ((0, 32),))
    return dict(tokens=tokens, d_mixed=d_mixed, route_ids=route_ids, route_weight=route_weight, gate_weight=gate_weight, up_weight=up_weight, down_weight=down_weight)


def slot_table(block_ids, expert_count):
    flat_ids = block_ids.reshape(-1)
    one_hot = (flat_ids[:, None] == jnp.arange(expert_count, dtype=jnp.int32)[None, :]).astype(jnp.int32)
    earlier = jnp.cumsum(one_hot, axis=0) - one_hot
    return jnp.sum(earlier * one_hot, axis=1).astype(jnp.int32)


def block_slots(block_ids):
    return slot_table(block_ids, EXPERTS)


def piece_pass(rows_in, rows_grad, gate_piece, up_piece, down_piece):
    gate_value = jnp.dot(rows_in, gate_piece.T, preferred_element_type=jnp.float32)
    up_value = jnp.dot(rows_in, up_piece.T, preferred_element_type=jnp.float32)
    sigmoid_gate = jax.nn.sigmoid(gate_value)
    activated = gate_value * sigmoid_gate
    hidden = (activated * up_value).astype(jnp.bfloat16)
    part_out = jnp.dot(hidden, down_piece, preferred_element_type=jnp.float32).astype(jnp.bfloat16)
    d_hidden = jnp.dot(rows_grad, down_piece.T, preferred_element_type=jnp.float32)
    grad_down = jnp.dot(hidden.T, rows_grad, preferred_element_type=jnp.float32).astype(jnp.bfloat16)
    d_gate_pre = (d_hidden * up_value * sigmoid_gate * (1.0 + gate_value * (1.0 - sigmoid_gate))).astype(jnp.bfloat16)
    d_up_pre = (d_hidden * activated).astype(jnp.bfloat16)
    grad_gate = jnp.dot(d_gate_pre.T, rows_in, preferred_element_type=jnp.float32).astype(jnp.bfloat16)
    grad_up = jnp.dot(d_up_pre.T, rows_in, preferred_element_type=jnp.float32).astype(jnp.bfloat16)
    part_in = (jnp.dot(d_gate_pre, gate_piece, preferred_element_type=jnp.float32)
               + jnp.dot(d_up_pre, up_piece, preferred_element_type=jnp.float32)).astype(jnp.bfloat16)
    return part_out, part_in, grad_gate, grad_up, grad_down


def expert_pass(packed):
    routed_in, routed_grad, gate_expert, up_expert, down_expert = packed
    rows_in = routed_in.reshape(N_DP * CAP, D)
    rows_grad = routed_grad.reshape(N_DP * CAP, D)
    total_out = jnp.zeros((N_DP * CAP, D), jnp.float32)
    total_in = jnp.zeros((N_DP * CAP, D), jnp.float32)
    gate_grads = []
    up_grads = []
    down_grads = []
    for position in range(PIECES):
        results = piece_pass(rows_in, rows_grad, gate_expert[position], up_expert[position], down_expert[position])
        total_out = total_out + results[0].astype(jnp.float32)
        total_in = total_in + results[1].astype(jnp.float32)
        gate_grads.append(results[2])
        up_grads.append(results[3])
        down_grads.append(results[4])
    return total_out, total_in, jnp.stack(gate_grads), jnp.stack(up_grads), jnp.stack(down_grads)


def reference(tokens, d_mixed, route_ids, route_weight, gate_weight, up_weight, down_weight):
    blocks = route_ids.reshape(N_DP, TOK_DEV, TOP)
    slot_numbers = jax.vmap(block_slots)(blocks).reshape(-1)
    flat_ids = route_ids.reshape(-1).astype(jnp.int32)
    flat_tokens = jnp.arange(TOKENS * TOP, dtype=jnp.int32) // TOP
    flat_blocks = flat_tokens // TOK_DEV
    flat_weight = route_weight.reshape(-1)
    routed_in = jnp.zeros((EXPERTS, N_DP, CAP, D), jnp.bfloat16)
    routed_in = routed_in.at[flat_ids, flat_blocks, slot_numbers].set(tokens[flat_tokens])
    grad_rows = (flat_weight[:, None] * d_mixed[flat_tokens].astype(jnp.float32)).astype(jnp.bfloat16)
    routed_grad = jnp.zeros((EXPERTS, N_DP, CAP, D), jnp.bfloat16)
    routed_grad = routed_grad.at[flat_ids, flat_blocks, slot_numbers].set(grad_rows)
    gate_all = gate_weight.reshape(EXPERTS, PIECES, HID, D)
    up_all = up_weight.reshape(EXPERTS, PIECES, HID, D)
    down_all = down_weight.reshape(EXPERTS, PIECES, HID, D)
    expert_out, expert_in, grad_gate, grad_up, grad_down = lax.map(
        expert_pass, (routed_in, routed_grad, gate_all, up_all, down_all))
    expert_out = expert_out.reshape(EXPERTS, N_DP, CAP, D)
    expert_in = expert_in.reshape(EXPERTS, N_DP, CAP, D)
    picked_out = expert_out[flat_ids, flat_blocks, slot_numbers].reshape(TOKENS, TOP, D)
    picked_in = expert_in[flat_ids, flat_blocks, slot_numbers].reshape(TOKENS, TOP, D)
    mixed = jnp.sum(route_weight[:, :, None] * picked_out, axis=1).astype(jnp.bfloat16)
    d_route = jnp.sum(picked_out * d_mixed.astype(jnp.float32)[:, None, :], axis=2)
    d_tokens = jnp.sum(picked_in, axis=1).astype(jnp.bfloat16)
    return (mixed, d_route, d_tokens,
            grad_gate.reshape(EXPERTS * PIECES, HID, D),
            grad_up.reshape(EXPERTS * PIECES, HID, D),
            grad_down.reshape(EXPERTS * PIECES, HID, D))
```

```python
import functools
import math

import jax
import jax.numpy as jnp
from jax import lax
from jax.experimental import pallas as pl
from jax.experimental.pallas import tpu as pltpu
from jax.sharding import PartitionSpec as P

EXP_DEV = 2
CORES = 2
MESH = pl.DeviceIdType.MESH
F32 = jnp.float32
BF16 = jnp.bfloat16


def dot(left, right, lhs_dim, rhs_dim):
    return lax.dot_general(
        left, right, (((lhs_dim,), (rhs_dim,)), ((), ())), preferred_element_type=F32
    )


def kernel(
    shape, tok, dmx, ids, wts, gate_hbm, up_hbm, down_hbm,
    mixed_out, route_out, dtok_out, ggate_out, gup_out, gdown_out,
    xs, ds, wg, wu, wd, gate, up, dhid, hw, dg, du,
    ps0, ps1, pr0, pr1, acc0, acc1, sb0, sb1, ra0, ra1, sc0, sc1, rb0, rb1,
    zb0, zb1, zf0, zf1, rz0, rz1, ag0, ag1, stage,
    send_sem, recv_sem, load_sem, store_sem,
):
    n_dp, side, n_z, rows, half, hid, row_parts, tile = shape
    ps, pr, acc, sb, ra = (ps0, ps1), (pr0, pr1), (acc0, acc1), (sb0, sb1), (ra0, ra1)
    sc, rb, zb, zf, rz, ag = (sc0, sc1), (rb0, rb1), (zb0, zb1), (zf0, zf1), (rz0, rz1), (ag0, ag1)
    dp = lax.axis_index("dp")
    column = lax.axis_index("expert")
    core = lax.rem(column, CORES)
    z = column // CORES
    step_a = 1 + core * (side - 1)
    step_b = side - core * (side - 1)
    a = lax.rem(dp // step_a, side)
    b = lax.rem(dp // step_b, side)

    def block_of(a_index, b_index):
        return a_index * step_a + b_index * step_b

    def turn(value, by, size):
        return lax.rem(value + by + size, size)

    sibling = (dp, column + 1 - 2 * core)

    def peer_a(by):
        return (block_of(turn(a, by, side), b), column)

    def peer_b(by):
        return (block_of(a, turn(b, by, side)), column)

    def peer_z(by):
        return (dp, turn(z, by, n_z) * CORES + core)

    partners = [sibling]
    partners += [peer_a(k) for k in range(1, side)]
    partners += [peer_b(k) for k in range(1, side)]
    partners += [peer_z(k) for k in range(1, n_z)]

    loads = []
    for number, (source, target) in enumerate(((gate_hbm, wg), (up_hbm, wu), (down_hbm, wd))):
        loads.append(pltpu.make_async_copy(source.at[0], target, load_sem.at[number]))
        loads[-1].start()

    used = [0]
    sent = []

    def send(source, target, device):
        copy = pltpu.make_async_remote_copy(
            src_ref=source, dst_ref=target, send_sem=send_sem.at[used[0]],
            recv_sem=recv_sem.at[used[0]], device_id=device, device_id_type=MESH,
        )
        used[0] += 1
        copy.start()
        sent.append(copy)
        return copy

    barrier = pltpu.get_barrier_semaphore()
    for partner in partners:
        pl.semaphore_signal(barrier, inc=1, device_id=partner, device_id_type=MESH)
    for part in range(CORES):
        xs[part, dp] = tok[:, part * half : (part + 1) * half]
        ds[part, dp] = dmx[:, part * half : (part + 1) * half]
    pl.semaphore_wait(barrier, len(partners))

    from_a, from_b, from_ab, from_core = [], [], [], []
    for buffer in (xs, ds):
        own = buffer.at[core, dp]
        from_a.append([send(own, own, peer_a(k)) for k in range(1, side)])
        from_b.append([send(own, own, peer_b(k)) for k in range(1, side)])
    for number, buffer in enumerate((xs, ds)):
        from_ab.append([])
        from_core.append([])
        for k in range(1, side):
            from_a[number][k - 1].wait_recv()
            got = buffer.at[core, block_of(turn(a, -k, side), b)]
            for m in range(1, side):
                from_ab[number].append(send(got, got, peer_b(m)))
            from_core[number].append(send(got, got, sibling))

    def finish_gather(number, buffer):
        for k in range(1, side):
            from_b[number][k - 1].wait_recv()
            got = buffer.at[core, block_of(a, turn(b, -k, side))]
            from_core[number].append(send(got, got, sibling))
        for k in range(1, side):
            for m in range(1, side):
                from_ab[number][(k - 1) * (side - 1) + m - 1].wait_recv()
                got = buffer.at[core, block_of(turn(a, -k, side), turn(b, -m, side))]
                from_core[number].append(send(got, got, sibling))

    def whole(buffer, part):
        return buffer[part].reshape(n_dp * rows, half)

    finish_gather(0, xs)
    for copy in from_core[0]:
        copy.wait_recv()
    loads[0].wait()
    gate[...] = dot(whole(xs, 0), wg[:, :half], 1, 1) + dot(whole(xs, 1), wg[:, half:], 1, 1)
    finish_gather(1, ds)
    loads[1].wait()
    up[...] = dot(whole(xs, 0), wu[:, :half], 1, 1) + dot(whole(xs, 1), wu[:, half:], 1, 1)
    for copy in from_core[1]:
        copy.wait_recv()
    loads[2].wait()
    dhid[...] = dot(whole(ds, 0), wd[:, :half], 1, 1) + dot(whole(ds, 1), wd[:, half:], 1, 1)

    pieces = n_dp // EXP_DEV
    expert = column * EXP_DEV + dp // pieces
    piece = lax.rem(dp, pieces)
    strip = rows // 2

    @pl.loop(0, 2 * n_dp)
    def elementwise(index):
        start = pl.multiple_of(index * strip, strip)
        span = pl.ds(start, strip)
        lane = lax.broadcasted_iota(jnp.int32, (strip, 128), 1)
        named = ids[span, :] == expert
        weight = jnp.sum(jnp.where(named & (lane < 8), wts[span, :], 0.0), axis=1, keepdims=True)
        gate_value = gate[span, :]
        up_value = up[span, :]
        plain = dhid[span, :]
        sigmoid_gate = 1.0 / (1.0 + jnp.exp(-gate_value))
        activated = gate_value * sigmoid_gate
        hidden = activated * up_value
        paired = jnp.sum(hidden * plain, axis=1, keepdims=True)
        d_hidden = weight * plain
        hw[span, :] = (weight * hidden).astype(BF16)
        dg[span, :] = (
            d_hidden * up_value * sigmoid_gate * (1.0 + gate_value * (1.0 - sigmoid_gate))
        ).astype(BF16)
        du[span, :] = (d_hidden * activated).astype(BF16)
        leading = paired.astype(BF16).astype(F32)
        share = jnp.where(lane < 64, leading, paired - leading)
        mine = named & (lax.rem(lane // 8, 8) == piece)
        block = index // 2
        inner = pl.ds(pl.multiple_of(lax.rem(index, 2) * strip, strip), strip)
        acc0[block, inner, half : half + 128] = jnp.where(mine, share, 0.0)
        if acc0.shape[2] > half + 128:
            acc0[block, inner, half + 128 :] = jnp.zeros(
                (strip, acc0.shape[2] - half - 128), F32
            )

    def product(which, columns):
        if which == 0:
            return dot(hw[...], wd[:, columns], 1, 0)
        return dot(dg[...], wg[:, columns], 1, 0) + dot(du[...], wu[:, columns], 1, 0)

    pair = []
    for q in range(2):

        @pl.loop(0, half // tile)
        def other_half(t, q=q):
            start = pl.multiple_of((1 - core) * half + t * tile, tile)
            value = product(q, pl.ds(start, tile)).astype(BF16)
            ps[q][:, :, pl.ds(pl.multiple_of(t * tile, tile), tile)] = value.reshape(
                n_dp, rows, tile
            )

        pair.append(send(ps[q], pr[q], sibling))

        @pl.loop(0, half // tile)
        def own_half(t, q=q):
            start = pl.multiple_of(core * half + t * tile, tile)
            value = product(q, pl.ds(start, tile))
            acc[q][:, :, pl.ds(pl.multiple_of(t * tile, tile), tile)] = value.reshape(
                n_dp, rows, tile
            )

    stores = []

    def weight_grad(number, left, buffer, target):
        for part in range(CORES):

            @pl.loop(0, half // tile)
            def columns(t, part=part):
                inner = pl.ds(pl.multiple_of(t * tile, tile), tile)
                right = buffer[part, :, :, inner].reshape(n_dp * rows, tile)
                start = pl.multiple_of(part * half + t * tile, tile)
                stage[number, :, pl.ds(start, tile)] = dot(left[...], right, 0, 0).astype(BF16)

        stores.append(pltpu.make_async_copy(stage.at[number], target.at[0], store_sem.at[number]))
        stores[-1].start()

    def pair_done(q):
        pair[q].wait_recv()

        @pl.loop(0, n_dp)
        def add(block):
            total = acc[q][block, :, :half] + pr[q][block].astype(F32)
            acc[q][block, :, :half] = total
            sb[q][block, :, :half] = total.astype(BF16)
            if acc[q].shape[2] > half:
                sb[q][block, :, half:] = acc[q][block, :, half:].astype(BF16)

        copies = []
        for k in range(1, side):
            for m in range(side):
                source = sb[q].at[block_of(turn(a, k, side), m)]
                copies.append(send(source, ra[q].at[k - 1, m], peer_a(k)))
        return copies

    def first_done(q, copies):
        for copy in copies:
            copy.wait_recv()
        following = []
        for m in range(1, side + 1):
            goal = turn(b, m, side)
            total = acc[q][block_of(a, goal)]
            for k in range(1, side):
                total = total + ra[q][k - 1, goal].astype(F32)
            if m < side:
                sc[q][m - 1] = total.astype(BF16)
                following.append(send(sc[q].at[m - 1], rb[q].at[m - 1], peer_b(m)))
            else:
                acc[q][block_of(a, b)] = total
        return following

    def second_done(q, copies):
        for copy in copies:
            copy.wait_recv()
        total = acc[q][block_of(a, b)]
        for k in range(1, side):
            total = total + rb[q][k - 1].astype(F32)
        high, wide = zb[q].shape[1:]
        for part in range(n_z):
            top = (part % row_parts) * high
            left = (part // row_parts) * wide
            value = total[top : top + high, left : left + wide]
            zf[q][part] = value
            zb[q][part] = value.astype(BF16)
        return [
            send(zb[q].at[turn(z, k, n_z)], rz[q].at[k - 1], peer_z(k)) for k in range(1, n_z)
        ]

    def third_done(q, copies):
        for copy in copies:
            copy.wait_recv()
        total = zf[q][z]
        for k in range(1, n_z):
            total = total + rz[q][k - 1].astype(F32)
        ag[q][core, z] = total.astype(BF16)
        own = ag[q].at[core, z]
        following = [send(own, own, peer_z(k)) for k in range(1, n_z)]
        return following, [send(own, own, sibling)]

    def fourth_done(q, copies, shared):
        for k in range(1, n_z):
            copies[k - 1].wait_recv()
            got = ag[q].at[core, turn(z, -k, n_z)]
            shared.append(send(got, got, sibling))

    first0 = pair_done(0)
    first1 = pair_done(1)
    weight_grad(0, hw, ds, gdown_out)
    second0 = first_done(0, first0)
    weight_grad(1, dg, xs, ggate_out)
    second1 = first_done(1, first1)
    third0 = second_done(0, second0)
    weight_grad(2, du, xs, gup_out)
    third1 = second_done(1, second1)
    fourth0, shared0 = third_done(0, third0)
    fourth1, shared1 = third_done(1, third1)
    fourth_done(0, fourth0, shared0)
    fourth_done(1, fourth1, shared1)

    for q, (target, shared) in enumerate(((mixed_out, shared0), (dtok_out, shared1))):
        for copy in shared:
            copy.wait_recv()
        high, wide = zb[q].shape[1:]
        routes = []
        for part in range(row_parts):
            span = slice(part * high, (part + 1) * high)
            for side_core in range(CORES):
                strips = [ag[q][side_core, k * row_parts + part] for k in range(n_z // row_parts)]
                line = strips[0] if len(strips) == 1 else jnp.concatenate(strips, axis=1)
                target[span, side_core * half : (side_core + 1) * half] = line[:, :half]
                if q == 0:
                    routes.append(line[:, half : half + 128].astype(F32))
            if q == 0:
                total = routes[-2] + routes[-1]
                for by in (64, 32, 16, 8):
                    total = total + pltpu.roll(total, by, 1)
                route_out[span, :] = total
    for copy in sent:
        copy.wait_send()
    for copy in stores:
        copy.wait()


def body(tokens, d_mixed, route_ids, route_weight, gate_weight, up_weight, down_weight):
    n_dp = lax.axis_size("dp")
    n_z = lax.axis_size("expert") // CORES
    side = math.isqrt(n_dp)
    rows, width = tokens.shape
    choices = route_ids.shape[1]
    hid = gate_weight.shape[1]
    half = width // CORES
    tile = 256
    row_parts = min(n_z, rows // 16)
    col_parts = n_z // row_parts
    high = rows // row_parts
    pad = ((0, 0), (0, 8 - choices))
    ids = jnp.tile(jnp.pad(route_ids, pad, constant_values=-1), (1, 16))
    wts = jnp.tile(jnp.pad(route_weight, pad), (1, 16))
    widths = (half + 128 * col_parts, half)
    total_rows = n_dp * rows

    def both(make):
        return [make(w) for w in widths]

    def vmem(*dims, dtype=BF16):
        return pltpu.VMEM(dims, dtype)

    scratch = [vmem(CORES, n_dp, rows, half)] * 2
    scratch += [vmem(hid, width)] * 3
    scratch += [vmem(total_rows, hid, dtype=F32)] * 3
    scratch += [vmem(total_rows, hid)] * 3
    scratch += [vmem(n_dp, rows, half)] * 4
    scratch += both(lambda w: vmem(n_dp, rows, w, dtype=F32))
    scratch += both(lambda w: vmem(n_dp, rows, w))
    scratch += both(lambda w: vmem(side - 1, side, rows, w))
    scratch += both(lambda w: vmem(side - 1, rows, w))
    scratch += both(lambda w: vmem(side - 1, rows, w))
    scratch += both(lambda w: vmem(n_z, high, w // col_parts))
    scratch += both(lambda w: vmem(n_z, high, w // col_parts, dtype=F32))
    scratch += both(lambda w: vmem(n_z - 1, high, w // col_parts))
    scratch += both(lambda w: vmem(CORES, n_z, high, w // col_parts))
    scratch += [vmem(3, hid, width)]
    gather = 2 * (2 * (side - 1) + (side - 1) ** 2 + n_dp - 1)
    reduce = 2 * (1 + (side - 1) * side + side - 1 + 2 * (n_z - 1) + n_z)
    copies = gather + reduce
    scratch += [pltpu.SemaphoreType.DMA((copies,))] * 2 + [pltpu.SemaphoreType.DMA((3,))] * 2

    in_vmem = pl.BlockSpec(memory_space=pltpu.VMEM)
    anywhere = pl.BlockSpec(memory_space=pl.ANY)
    grad = jax.ShapeDtypeStruct((1, hid, width), BF16)
    flat = jax.ShapeDtypeStruct((rows, width), BF16)
    shape = (n_dp, side, n_z, rows, half, hid, row_parts, tile)
    mixed, route, d_tokens, grad_gate, grad_up, grad_down = pl.pallas_call(
        functools.partial(kernel, shape),
        out_shape=(flat, jax.ShapeDtypeStruct((rows, 128), F32), flat, grad, grad, grad),
        in_specs=[in_vmem] * 4 + [anywhere] * 3,
        out_specs=(in_vmem,) * 3 + (anywhere,) * 3,
        scratch_shapes=scratch,
        compiler_params=pltpu.CompilerParams(
            collective_id=0, has_side_effects=True, vmem_limit_bytes=60 * 1024 * 1024
        ),
        cost_estimate=pl.CostEstimate(
            flops=18 * total_rows * hid * width,
            bytes_accessed=12 * hid * width,
            transcendentals=total_rows * hid,
        ),
    )(tokens, d_mixed, ids, wts, gate_weight, up_weight, down_weight)
    return mixed, route[:, :choices], d_tokens, grad_gate, grad_up, grad_down


def solution(mesh):
    row, whole, block = P("dp", None), P(), P(("expert", "dp"), None, None)
    return jax.shard_map(
        body,
        mesh=mesh,
        in_specs=(row, row, whole, whole, block, block, block),
        out_specs=(row, row, row, block, block, block),
        check_vma=False,
    )
```

```python
import functools
import math

import jax
import jax.numpy as jnp
from jax import lax
from jax.experimental import pallas as pl
from jax.experimental.pallas import tpu as pltpu
from jax.sharding import PartitionSpec as P

EXP_DEV = 2
CORES = 2
MESH = pl.DeviceIdType.MESH
F32 = jnp.float32
BF16 = jnp.bfloat16


def dot(left, right, lhs_dim, rhs_dim):
    return lax.dot_general(
        left, right, (((lhs_dim,), (rhs_dim,)), ((), ())), preferred_element_type=F32
    )


def kernel(
    shape, tok, dmx, ids, wts, gate_hbm, up_hbm, down_hbm,
    mixed_out, route_out, dtok_out, xs_out, ds_out, hw_out, dg_out, du_out, *scratch,
):
    n_dp, side, n_z, rows, half, row_parts, tile, chunks = shape
    scratch = list(scratch)

    def take(count):
        taken = scratch[:count]
        del scratch[:count]
        return taken

    xs, ds, wg, wu, wd, gate, up, hidf, dhid, hw, dg, du, mine, weight_of = take(14)
    turned = take(3)
    count = len(chunks)
    ps, pr, acc, sb, ra, sc, rb, zb, zf, rz, ag = [take(count) for _ in range(11)]
    send_sem, recv_sem, load_sem, store_sem = take(4)
    dp = lax.axis_index("dp")
    column = lax.axis_index("expert")
    core = lax.rem(column, CORES)
    z = column // CORES
    step_a = 1 + core * (side - 1)
    step_b = side - core * (side - 1)
    a = lax.rem(dp // step_a, side)
    b = lax.rem(dp // step_b, side)

    def block_of(a_index, b_index):
        return a_index * step_a + b_index * step_b

    def turn(value, by, size):
        return lax.rem(value + by + size, size)

    sibling = (dp, column + 1 - 2 * core)

    def peer_a(by):
        return (block_of(turn(a, by, side), b), column)

    def peer_b(by):
        return (block_of(a, turn(b, by, side)), column)

    def peer_z(by):
        return (dp, turn(z, by, n_z) * CORES + core)

    partners = [sibling]
    partners += [peer_a(k) for k in range(1, side)]
    partners += [peer_b(k) for k in range(1, side)]
    partners += [peer_z(k) for k in range(1, n_z)]

    loads = []
    for number, (source, target) in enumerate(((gate_hbm, wg), (up_hbm, wu), (down_hbm, wd))):
        loads.append(pltpu.make_async_copy(source.at[0], target, load_sem.at[number]))
        loads[-1].start()

    used = [0]
    sent = []

    def send(source, target, device):
        copy = pltpu.make_async_remote_copy(
            src_ref=source, dst_ref=target, send_sem=send_sem.at[used[0]],
            recv_sem=recv_sem.at[used[0]], device_id=device, device_id_type=MESH,
        )
        used[0] += 1
        copy.start()
        sent.append(copy)
        return copy

    barrier = pltpu.get_barrier_semaphore()
    for partner in partners:
        pl.semaphore_signal(barrier, inc=1, device_id=partner, device_id_type=MESH)
    for part in range(CORES):
        xs[part, dp] = tok[:, part * half : (part + 1) * half]
        ds[part, dp] = dmx[:, part * half : (part + 1) * half]
    pl.semaphore_wait(barrier, len(partners))

    from_a, from_b, from_ab, from_core = [], [], [], []
    for buffer in (xs, ds):
        own = buffer.at[core, dp]
        from_a.append([send(own, own, peer_a(k)) for k in range(1, side)])
        from_b.append([send(own, own, peer_b(k)) for k in range(1, side)])
    for number, buffer in enumerate((xs, ds)):
        from_ab.append([])
        from_core.append([])
        for k in range(1, side):
            from_a[number][k - 1].wait_recv()
            got = buffer.at[core, block_of(turn(a, -k, side), b)]
            for m in range(1, side):
                from_ab[number].append(send(got, got, peer_b(m)))
            from_core[number].append(send(got, got, sibling))

    def finish_gather(number, buffer):
        for k in range(1, side):
            from_b[number][k - 1].wait_recv()
            got = buffer.at[core, block_of(a, turn(b, -k, side))]
            from_core[number].append(send(got, got, sibling))
        for k in range(1, side):
            for m in range(1, side):
                from_ab[number][(k - 1) * (side - 1) + m - 1].wait_recv()
                got = buffer.at[core, block_of(turn(a, -k, side), turn(b, -m, side))]
                from_core[number].append(send(got, got, sibling))

    def whole(buffer, part):
        return buffer[part].reshape(n_dp * rows, half)

    pieces = n_dp // EXP_DEV
    expert = column * EXP_DEV + dp // pieces
    piece = lax.rem(dp, pieces)
    choices = ids.shape[0]
    spread = (
        lax.rem(lax.broadcasted_iota(jnp.int32, (choices, 128), 1), 8)
        == lax.broadcasted_iota(jnp.int32, (choices, 128), 0)
    ).astype(F32)

    def spread_lanes(value):
        return lax.dot_general(
            value, spread, (((0,), (0,)), ((), ())),
            precision=lax.Precision.HIGHEST, preferred_element_type=F32,
        )

    lanes = lax.broadcasted_iota(jnp.int32, (n_dp * rows, 128), 1)
    hit = ids[...] == expert
    named = spread_lanes(hit.astype(F32))
    weight_of[...] = jnp.broadcast_to(
        jnp.sum(
            jnp.where(lanes < 8, spread_lanes(jnp.where(hit, wts[...], 0.0)), 0.0),
            axis=1, keepdims=True,
        ),
        (n_dp * rows, 128),
    )
    mine[...] = jnp.where(lax.rem(lanes // 8, 8) == piece, named, 0.0)

    stores = []

    def keep(source, target):
        stores.append(pltpu.make_async_copy(source, target, store_sem.at[len(stores)]))
        stores[-1].start()

    finish_gather(0, xs)
    for copy in from_core[0]:
        copy.wait_recv()
    loads[0].wait()
    gate[...] = dot(whole(xs, 0), wg[:, :half], 1, 1) + dot(whole(xs, 1), wg[:, half:], 1, 1)
    finish_gather(1, ds)
    loads[1].wait()
    up[...] = dot(whole(xs, 0), wu[:, :half], 1, 1) + dot(whole(xs, 1), wu[:, half:], 1, 1)
    strip = rows // 2

    @pl.loop(0, 2 * n_dp)
    def forward(index):
        span = pl.ds(pl.multiple_of(index * strip, strip), strip)
        gate_value = gate[span, :]
        up_value = up[span, :]
        sigmoid_gate = 1.0 / (1.0 + jnp.exp(-gate_value))
        activated = gate_value * sigmoid_gate
        hidden = activated * up_value
        hw[span, :] = (weight_of[span, :1] * hidden).astype(BF16)
        hidf[span, :] = hidden
        up[span, :] = activated
        gate[span, :] = up_value * sigmoid_gate * (1.0 + gate_value * (1.0 - sigmoid_gate))

    def product(q, columns):
        if q == 0:
            return dot(hw[...], wd[:, columns], 1, 0)
        return dot(dg[...], wg[:, columns], 1, 0) + dot(du[...], wu[:, columns], 1, 0)

    def other_half(q):
        first, wide = chunks[q]

        @pl.loop(0, wide // tile)
        def columns(t):
            start = pl.multiple_of((1 - core) * half + first + t * tile, tile)
            value = product(q, pl.ds(start, tile)).astype(BF16)
            ps[q][:, :, pl.ds(pl.multiple_of(t * tile, tile), tile)] = value.reshape(
                n_dp, rows, tile
            )

        return send(ps[q], pr[q], sibling)

    def own_half(q):
        first, wide = chunks[q]

        @pl.loop(0, wide // tile)
        def columns(t):
            start = pl.multiple_of(core * half + first + t * tile, tile)
            value = product(q, pl.ds(start, tile))
            acc[q][:, :, pl.ds(pl.multiple_of(t * tile, tile), tile)] = value.reshape(
                n_dp, rows, tile
            )

    def pair_done(q, copy):
        copy.wait_recv()
        wide = chunks[q][1]

        @pl.loop(0, n_dp)
        def add(block):
            total = acc[q][block, :, :wide] + pr[q][block].astype(F32)
            acc[q][block, :, :wide] = total
            sb[q][block, :, :wide] = total.astype(BF16)
            if acc[q].shape[2] > wide:
                sb[q][block, :, wide:] = acc[q][block, :, wide:].astype(BF16)

        copies = []
        for k in range(1, side):
            for m in range(side):
                source = sb[q].at[block_of(turn(a, k, side), m)]
                copies.append(send(source, ra[q].at[k - 1, m], peer_a(k)))
        return copies

    def first_done(q, copies):
        for copy in copies:
            copy.wait_recv()
        following = []
        for m in range(1, side + 1):
            goal = turn(b, m, side)
            total = acc[q][block_of(a, goal)]
            for k in range(1, side):
                total = total + ra[q][k - 1, goal].astype(F32)
            if m < side:
                sc[q][m - 1] = total.astype(BF16)
                following.append(send(sc[q].at[m - 1], rb[q].at[m - 1], peer_b(m)))
            else:
                acc[q][block_of(a, b)] = total
        return following

    def second_done(q, copies):
        for copy in copies:
            copy.wait_recv()
        total = acc[q][block_of(a, b)]
        for k in range(1, side):
            total = total + rb[q][k - 1].astype(F32)
        high, wide = zb[q].shape[1:]
        for part in range(n_z):
            top = (part % row_parts) * high
            left = (part // row_parts) * wide
            value = total[top : top + high, left : left + wide]
            zf[q][part] = value
            zb[q][part] = value.astype(BF16)
        return [
            send(zb[q].at[turn(z, k, n_z)], rz[q].at[k - 1], peer_z(k)) for k in range(1, n_z)
        ]

    def third_done(q, copies):
        for copy in copies:
            copy.wait_recv()
        total = zf[q][z]
        for k in range(1, n_z):
            total = total + rz[q][k - 1].astype(F32)
        ag[q][core, z] = total.astype(BF16)
        own = ag[q].at[core, z]
        following = [send(own, own, peer_z(k)) for k in range(1, n_z)]
        return following, [send(own, own, sibling)]

    def fourth_done(q, copies, shared):
        for k in range(1, n_z):
            copies[k - 1].wait_recv()
            got = ag[q].at[core, turn(z, -k, n_z)]
            shared.append(send(got, got, sibling))

    loads[2].wait()
    pair0 = other_half(0)
    own_half(0)
    step0 = pair_done(0, pair0)
    for copy in from_core[1]:
        copy.wait_recv()
    dhid[...] = dot(whole(ds, 0), wd[:, :half], 1, 1) + dot(whole(ds, 1), wd[:, half:], 1, 1)

    @pl.loop(0, 2 * n_dp)
    def backward(index):
        span = pl.ds(pl.multiple_of(index * strip, strip), strip)
        lane = lax.broadcasted_iota(jnp.int32, (strip, 128), 1)
        plain = dhid[span, :]
        paired = jnp.sum(hidf[span, :] * plain, axis=1, keepdims=True)
        d_hidden = weight_of[span, :1] * plain
        dg[span, :] = (d_hidden * gate[span, :]).astype(BF16)
        du[span, :] = (d_hidden * up[span, :]).astype(BF16)
        leading = paired.astype(BF16).astype(F32)
        share = jnp.where(lane < 64, leading, paired - leading) * mine[span, :]
        block = index // 2
        inner = pl.ds(pl.multiple_of(lax.rem(index, 2) * strip, strip), strip)
        wide = chunks[1][1]
        acc[1][block, inner, wide : wide + 128] = share
        if acc[1].shape[2] > wide + 128:
            acc[1][block, inner, wide + 128 :] = jnp.zeros(
                (strip, acc[1].shape[2] - wide - 128), F32
            )

    pair1 = other_half(1)
    step0 = first_done(0, step0)
    own_half(1)
    step1 = pair_done(1, pair1)
    pair2 = other_half(2)
    step0 = second_done(0, step0)
    own_half(2)
    step2 = pair_done(2, pair2)
    step1 = first_done(1, step1)
    keep(xs, xs_out)
    keep(ds, ds_out)
    for number, (source, target) in enumerate(((hw, hw_out), (dg, dg_out), (du, du_out))):
        turned[number][...] = jnp.transpose(source[...])
        keep(turned[number], target)
    step0, shared0 = third_done(0, step0)
    step2 = first_done(2, step2)
    step1 = second_done(1, step1)
    step2 = second_done(2, step2)
    fourth_done(0, step0, shared0)
    step1, shared1 = third_done(1, step1)
    step2, shared2 = third_done(2, step2)
    fourth_done(1, step1, shared1)
    fourth_done(2, step2, shared2)

    for q, (target, shared) in enumerate(
        ((mixed_out, shared0), (dtok_out, shared1), (dtok_out, shared2))
    ):
        for copy in shared:
            copy.wait_recv()
        first, width = chunks[q]
        high = zb[q].shape[1]
        for part in range(row_parts):
            span = slice(part * high, (part + 1) * high)
            routes = 0.0
            for side_core in range(CORES):
                strips = [ag[q][side_core, k * row_parts + part] for k in range(n_z // row_parts)]
                line = strips[0] if len(strips) == 1 else jnp.concatenate(strips, axis=1)
                left = side_core * half + first
                target[span, left : left + width] = line[:, :width]
                if q == 1:
                    routes = routes + line[:, width : width + 128].astype(F32)
            if q == 1:
                for by in (64, 32, 16, 8):
                    routes = routes + pltpu.roll(routes, by, 1)
                route_out[span, :] = routes
    for copy in sent:
        copy.wait_send()
    for copy in stores:
        copy.wait()


def finish(mixed, route, d_tokens, xs, ds, hw, dg, du, mixed_out, route_out, dtok_out, gg, gu, gd):
    @pl.when(pl.program_id(0) == 0)
    def once():
        mixed_out[...] = mixed[...]
        dtok_out[...] = d_tokens[...]
        route_out[...] = jnp.transpose(route[...])[: route_out.shape[0]]

    total_rows = hw.shape[1]
    x_tile = xs[0].reshape(total_rows, xs.shape[3])
    d_tile = ds[0].reshape(total_rows, ds.shape[3])
    gd[0] = dot(hw[...], d_tile, 1, 0).astype(BF16)
    gg[0] = dot(dg[...], x_tile, 1, 0).astype(BF16)
    gu[0] = dot(du[...], x_tile, 1, 0).astype(BF16)


def body(tokens, d_mixed, route_ids, route_weight, gate_weight, up_weight, down_weight):
    n_dp = lax.axis_size("dp")
    n_z = lax.axis_size("expert") // CORES
    side = math.isqrt(n_dp)
    rows, width = tokens.shape
    choices = route_ids.shape[1]
    hid = gate_weight.shape[1]
    half = width // CORES
    tile = 256
    row_parts = min(n_z, rows // 16)
    col_parts = n_z // row_parts
    high = rows // row_parts
    chunks = ((0, half), (0, half // 2), (half // 2, half // 2))
    plain_widths = tuple(wide for _, wide in chunks)
    widths = (half, half // 2 + 128 * col_parts, half // 2)
    total_rows = n_dp * rows

    def vmem(*dims, dtype=BF16):
        return pltpu.VMEM(dims, dtype)

    def each(make, sizes=widths):
        return [make(w) for w in sizes]

    scratch = [vmem(CORES, n_dp, rows, half)] * 2
    scratch += [vmem(hid, width)] * 3
    scratch += [vmem(total_rows, hid, dtype=F32)] * 4
    scratch += [vmem(total_rows, hid)] * 3
    scratch += [vmem(total_rows, 128, dtype=F32)] * 2
    scratch += [vmem(hid, total_rows)] * 3
    scratch += each(lambda w: vmem(n_dp, rows, w), plain_widths) * 2
    scratch += each(lambda w: vmem(n_dp, rows, w, dtype=F32))
    scratch += each(lambda w: vmem(n_dp, rows, w))
    scratch += each(lambda w: vmem(side - 1, side, rows, w))
    scratch += each(lambda w: vmem(side - 1, rows, w))
    scratch += each(lambda w: vmem(side - 1, rows, w))
    scratch += each(lambda w: vmem(n_z, high, w // col_parts))
    scratch += each(lambda w: vmem(n_z, high, w // col_parts, dtype=F32))
    scratch += each(lambda w: vmem(n_z - 1, high, w // col_parts))
    scratch += each(lambda w: vmem(CORES, n_z, high, w // col_parts))
    gather = 2 * (2 * (side - 1) + (side - 1) ** 2 + n_dp - 1)
    reduce = len(chunks) * (1 + (side - 1) * side + side - 1 + 2 * (n_z - 1) + n_z)
    copies = gather + reduce
    scratch += [pltpu.SemaphoreType.DMA((copies,))] * 2
    scratch += [pltpu.SemaphoreType.DMA((3,)), pltpu.SemaphoreType.DMA((5,))]

    in_vmem = pl.BlockSpec(memory_space=pltpu.VMEM)
    anywhere = pl.BlockSpec(memory_space=pl.ANY)
    flat = jax.ShapeDtypeStruct((rows, width), BF16)
    gathered = jax.ShapeDtypeStruct((CORES, n_dp, rows, half), BF16)
    left = jax.ShapeDtypeStruct((hid, total_rows), BF16)
    shape = (n_dp, side, n_z, rows, half, row_parts, tile, chunks)
    results = pl.pallas_call(
        functools.partial(kernel, shape),
        out_shape=(flat, jax.ShapeDtypeStruct((rows, 128), F32), flat)
        + (gathered,) * 2 + (left,) * 3,
        in_specs=[in_vmem] * 4 + [anywhere] * 3,
        out_specs=(in_vmem,) * 3 + (anywhere,) * 5,
        scratch_shapes=scratch,
        compiler_params=pltpu.CompilerParams(
            collective_id=0, has_side_effects=True, vmem_limit_bytes=60 * 1024 * 1024
        ),
        cost_estimate=pl.CostEstimate(
            flops=12 * total_rows * hid * width,
            bytes_accessed=6 * hid * width,
            transcendentals=total_rows * hid,
        ),
    )(tokens, d_mixed, route_ids.T, route_weight.T, gate_weight, up_weight, down_weight)

    per_half = half // tile

    def fixed(*dims):
        return pl.BlockSpec(dims, lambda j: (0,) * len(dims))

    rows_tile = pl.BlockSpec(
        (1, n_dp, rows, tile), lambda j: (j // per_half, 0, 0, lax.rem(j, per_half))
    )
    grad_tile = pl.BlockSpec((1, hid, tile), lambda j: (0, 0, j))
    grad = jax.ShapeDtypeStruct((1, hid, width), BF16)
    mixed, route, d_tokens, grad_gate, grad_up, grad_down = pl.pallas_call(
        finish,
        grid=(width // tile,),
        out_shape=(flat, jax.ShapeDtypeStruct((choices, rows), F32), flat, grad, grad, grad),
        in_specs=[fixed(rows, width), fixed(rows, 128), fixed(rows, width)]
        + [rows_tile] * 2 + [fixed(hid, total_rows)] * 3,
        out_specs=(fixed(rows, width), fixed(choices, rows), fixed(rows, width))
        + (grad_tile,) * 3,
        compiler_params=pltpu.CompilerParams(vmem_limit_bytes=60 * 1024 * 1024),
        cost_estimate=pl.CostEstimate(
            flops=6 * total_rows * hid * width,
            bytes_accessed=6 * hid * width,
            transcendentals=0,
        ),
    )(*results)
    return mixed, route.T, d_tokens, grad_gate, grad_up, grad_down


def solution(mesh):
    row, whole, block = P("dp", None), P(), P(("expert", "dp"), None, None)
    return jax.shard_map(
        body,
        mesh=mesh,
        in_specs=(row, row, whole, whole, block, block, block),
        out_specs=(row, row, row, block, block, block),
        check_vma=False,
    )
```

```python
import functools
import math

import jax
import jax.numpy as jnp
from jax import lax
from jax.experimental import pallas as pl
from jax.experimental.pallas import tpu as pltpu
from jax.sharding import PartitionSpec as P

EXP_DEV = 2
CORES = 2
MESH = pl.DeviceIdType.MESH
F32 = jnp.float32
BF16 = jnp.bfloat16


def dot(left, right, lhs_dim, rhs_dim):
    return lax.dot_general(
        left, right, (((lhs_dim,), (rhs_dim,)), ((), ())), preferred_element_type=F32
    )


def kernel(
    shape, tok, dmx, ids, wts, gate_hbm, up_hbm, down_hbm,
    mixed_out, route_out, dtok_out, xs_out, ds_out, hw_out, dg_out, du_out, *scratch,
):
    n_dp, side, n_z, rows, half, row_parts, tile, chunks = shape
    scratch = list(scratch)

    def take(count):
        taken = scratch[:count]
        del scratch[:count]
        return taken

    xs, ds, wg, wu, wd, gate, up, hidf, dhid, ids8, wts8, paired = take(12)
    turned = take(3)
    hw, dg, du = take(3)
    count = len(chunks)
    ps, pr, acc, sb, ra, sc, rb, zb, zf, rz, ag = [take(count) for _ in range(11)]
    send_sem, recv_sem, load_sem, store_sem = take(4)
    dp = lax.axis_index("dp")
    column = lax.axis_index("expert")
    core = lax.rem(column, CORES)
    z = column // CORES
    step_a = 1 + core * (side - 1)
    step_b = side - core * (side - 1)
    a = lax.rem(dp // step_a, side)
    b = lax.rem(dp // step_b, side)

    def block_of(a_index, b_index):
        return a_index * step_a + b_index * step_b

    def turn(value, by, size):
        return lax.rem(value + by + size, size)

    sibling = (dp, column + 1 - 2 * core)

    def peer_a(by):
        return (block_of(turn(a, by, side), b), column)

    def peer_b(by):
        return (block_of(a, turn(b, by, side)), column)

    def peer_z(by):
        return (dp, turn(z, by, n_z) * CORES + core)

    partners = [sibling]
    partners += [peer_a(k) for k in range(1, side)]
    partners += [peer_b(k) for k in range(1, side)]
    partners += [peer_z(k) for k in range(1, n_z)]

    loads = []
    for number, (source, target) in enumerate(((gate_hbm, wg), (up_hbm, wu), (down_hbm, wd))):
        loads.append(pltpu.make_async_copy(source.at[0], target, load_sem.at[number]))
        loads[-1].start()

    used = [0]
    sent = []

    def send(source, target, device):
        copy = pltpu.make_async_remote_copy(
            src_ref=source, dst_ref=target, send_sem=send_sem.at[used[0]],
            recv_sem=recv_sem.at[used[0]], device_id=device, device_id_type=MESH,
        )
        used[0] += 1
        copy.start()
        sent.append(copy)
        return copy

    barrier = pltpu.get_barrier_semaphore()
    for partner in partners:
        pl.semaphore_signal(barrier, inc=1, device_id=partner, device_id_type=MESH)
    for part in range(CORES):
        xs[part, dp] = tok[:, part * half : (part + 1) * half]
        ds[part, dp] = dmx[:, part * half : (part + 1) * half]
    pl.semaphore_wait(barrier, len(partners))

    from_a, from_b, from_ab, from_core = [], [], [], []

    def pass_on(number, buffer):
        from_ab.append([])
        from_core.append([])
        for k in range(1, side):
            from_a[number][k - 1].wait_recv()
            got = buffer.at[core, block_of(turn(a, -k, side), b)]
            for m in range(1, side):
                from_ab[number].append(send(got, got, peer_b(m)))
            from_core[number].append(send(got, got, sibling))

    for buffer in (xs, ds):
        own = buffer.at[core, dp]
        from_a.append([send(own, own, peer_a(k)) for k in range(1, side)])
        from_b.append([send(own, own, peer_b(k)) for k in range(1, side)])
        if buffer is xs:
            pass_on(0, xs)

    def finish_gather(number, buffer):
        for k in range(1, side):
            from_b[number][k - 1].wait_recv()
            got = buffer.at[core, block_of(a, turn(b, -k, side))]
            from_core[number].append(send(got, got, sibling))
        for k in range(1, side):
            for m in range(1, side):
                from_ab[number][(k - 1) * (side - 1) + m - 1].wait_recv()
                got = buffer.at[core, block_of(turn(a, -k, side), turn(b, -m, side))]
                from_core[number].append(send(got, got, sibling))

    def whole(buffer, part):
        return buffer[part].reshape(n_dp * rows, half)

    pieces = n_dp // EXP_DEV
    expert = column * EXP_DEV + dp // pieces
    piece = lax.rem(dp, pieces)
    choices = ids.shape[0]
    ids8[...] = jnp.full(ids8.shape, -1, jnp.int32)
    ids8[:choices, :] = ids[...]
    wts8[...] = jnp.zeros(wts8.shape, F32)
    wts8[:choices, :] = wts[...]
    named = ids8[...] == expert
    weight = jnp.sum(jnp.where(named, wts8[...], 0.0), axis=0, keepdims=True)

    stores = []

    def keep(source, target):
        stores.append(pltpu.make_async_copy(source, target, store_sem.at[len(stores)]))
        stores[-1].start()

    finish_gather(0, xs)
    for copy in from_core[0]:
        copy.wait_recv()
    loads[0].wait()
    gate[...] = dot(wg[:, :half], whole(xs, 0), 1, 1) + dot(wg[:, half:], whole(xs, 1), 1, 1)
    pass_on(1, ds)
    loads[1].wait()
    up[...] = dot(wu[:, :half], whole(xs, 0), 1, 1) + dot(wu[:, half:], whole(xs, 1), 1, 1)
    hid = gate.shape[0]
    strip = 16 * max(k for k in range(1, 12) if hid // 16 % k == 0)

    @pl.loop(0, hid // strip)
    def forward(index):
        span = pl.ds(pl.multiple_of(index * strip, strip), strip)
        gate_value = gate[span, :]
        up_value = up[span, :]
        sigmoid_gate = 1.0 / (1.0 + jnp.exp(-gate_value))
        activated = gate_value * sigmoid_gate
        hidden = activated * up_value
        turned[0][span, :] = (weight * hidden).astype(BF16)
        hidf[span, :] = hidden
        up[span, :] = activated
        gate[span, :] = up_value * sigmoid_gate * (1.0 + gate_value * (1.0 - sigmoid_gate))

    hw[...] = jnp.transpose(turned[0][...])

    def product(q, columns):
        if q == 0:
            return dot(hw[...], wd[:, columns], 1, 0)
        return dot(dg[...], wg[:, columns], 1, 0) + dot(du[...], wu[:, columns], 1, 0)

    def other_half(q):
        first, wide = chunks[q]

        @pl.loop(0, wide // tile)
        def columns(t):
            start = pl.multiple_of((1 - core) * half + first + t * tile, tile)
            value = product(q, pl.ds(start, tile)).astype(BF16)
            ps[q][:, :, pl.ds(pl.multiple_of(t * tile, tile), tile)] = value.reshape(
                n_dp, rows, tile
            )

        return send(ps[q], pr[q], sibling)

    def own_half(q):
        first, wide = chunks[q]

        @pl.loop(0, wide // tile)
        def columns(t):
            start = pl.multiple_of(core * half + first + t * tile, tile)
            value = product(q, pl.ds(start, tile))
            acc[q][:, :, pl.ds(pl.multiple_of(t * tile, tile), tile)] = value.reshape(
                n_dp, rows, tile
            )

    def pair_done(q, copy):
        copy.wait_recv()
        wide = chunks[q][1]

        @pl.loop(0, n_dp)
        def add(block):
            total = acc[q][block, :, :wide] + pr[q][block].astype(F32)
            acc[q][block, :, :wide] = total
            sb[q][block, :, :wide] = total.astype(BF16)
            if acc[q].shape[2] > wide:
                sb[q][block, :, wide:] = acc[q][block, :, wide:].astype(BF16)

        copies = []
        for k in range(1, side):
            for m in range(side):
                source = sb[q].at[block_of(turn(a, k, side), m)]
                copies.append(send(source, ra[q].at[k - 1, m], peer_a(k)))
        return copies

    def first_done(q, copies):
        for copy in copies:
            copy.wait_recv()
        following = []
        for m in range(1, side + 1):
            goal = turn(b, m, side)
            total = acc[q][block_of(a, goal)]
            for k in range(1, side):
                total = total + ra[q][k - 1, goal].astype(F32)
            if m < side:
                sc[q][m - 1] = total.astype(BF16)
                following.append(send(sc[q].at[m - 1], rb[q].at[m - 1], peer_b(m)))
            else:
                acc[q][block_of(a, b)] = total
        return following

    def second_done(q, copies):
        for copy in copies:
            copy.wait_recv()
        total = acc[q][block_of(a, b)]
        for k in range(1, side):
            total = total + rb[q][k - 1].astype(F32)
        high, wide = zb[q].shape[1:]
        for part in range(n_z):
            top = (part % row_parts) * high
            left = (part // row_parts) * wide
            value = total[top : top + high, left : left + wide]
            zf[q][part] = value
            zb[q][part] = value.astype(BF16)
        return [
            send(zb[q].at[turn(z, k, n_z)], rz[q].at[k - 1], peer_z(k)) for k in range(1, n_z)
        ]

    def third_done(q, copies):
        for copy in copies:
            copy.wait_recv()
        total = zf[q][z]
        for k in range(1, n_z):
            total = total + rz[q][k - 1].astype(F32)
        ag[q][core, z] = total.astype(BF16)
        own = ag[q].at[core, z]
        following = [send(own, own, peer_z(k)) for k in range(1, n_z)]
        return following, [send(own, own, sibling)]

    def fourth_done(q, copies, shared):
        for k in range(1, n_z):
            copies[k - 1].wait_recv()
            got = ag[q].at[core, turn(z, -k, n_z)]
            shared.append(send(got, got, sibling))

    loads[2].wait()
    pair0 = other_half(0)
    finish_gather(1, ds)
    own_half(0)
    step0 = pair_done(0, pair0)
    for copy in from_core[1]:
        copy.wait_recv()
    dhid[...] = dot(wd[:, :half], whole(ds, 0), 1, 1) + dot(wd[:, half:], whole(ds, 1), 1, 1)
    paired[...] = jnp.zeros(paired.shape, F32)

    @pl.loop(0, hid // strip)
    def backward(index):
        span = pl.ds(pl.multiple_of(index * strip, strip), strip)
        plain = dhid[span, :]
        paired[...] += jnp.sum(hidf[span, :] * plain, axis=0, keepdims=True)
        d_hidden = weight * plain
        turned[1][span, :] = (d_hidden * gate[span, :]).astype(BF16)
        turned[2][span, :] = (d_hidden * up[span, :]).astype(BF16)

    dg[...] = jnp.transpose(turned[1][...])
    du[...] = jnp.transpose(turned[2][...])
    share = paired[...]
    leading = share.astype(BF16).astype(F32)
    kept = jnp.where(named, leading, 0.0)
    rest = jnp.where(named, share - leading, 0.0)
    groups = [jnp.where(piece == k, kept, 0.0) for k in range(8)]
    groups += [jnp.where(piece == k, rest, 0.0) for k in range(8)]
    lanes = jnp.transpose(jnp.concatenate(groups, axis=0)).reshape(n_dp, rows, 128)
    wide = chunks[1][1]
    acc[1][:, :, wide : wide + 128] = lanes
    extra = acc[1].shape[2] - wide - 128
    if extra:
        acc[1][:, :, wide + 128 :] = jnp.zeros((n_dp, rows, extra), F32)

    pair1 = other_half(1)
    step0 = first_done(0, step0)
    own_half(1)
    step1 = pair_done(1, pair1)
    pair2 = other_half(2)
    step0 = second_done(0, step0)
    own_half(2)
    step2 = pair_done(2, pair2)
    step1 = first_done(1, step1)
    keep(xs, xs_out)
    keep(ds, ds_out)
    for source, target in zip(turned, (hw_out, dg_out, du_out)):
        keep(source, target)
    step0, shared0 = third_done(0, step0)
    step2 = first_done(2, step2)
    step1 = second_done(1, step1)
    step2 = second_done(2, step2)
    fourth_done(0, step0, shared0)
    step1, shared1 = third_done(1, step1)
    step2, shared2 = third_done(2, step2)
    fourth_done(1, step1, shared1)
    fourth_done(2, step2, shared2)

    for q, (target, shared) in enumerate(
        ((mixed_out, shared0), (dtok_out, shared1), (dtok_out, shared2))
    ):
        for copy in shared:
            copy.wait_recv()
        first, width = chunks[q]
        high = zb[q].shape[1]
        for part in range(row_parts):
            span = slice(part * high, (part + 1) * high)
            routes = 0.0
            for side_core in range(CORES):
                strips = [ag[q][side_core, k * row_parts + part] for k in range(n_z // row_parts)]
                line = strips[0] if len(strips) == 1 else jnp.concatenate(strips, axis=1)
                left = side_core * half + first
                target[span, left : left + width] = line[:, :width]
                if q == 1:
                    routes = routes + line[:, width : width + 128].astype(F32)
            if q == 1:
                for by in (64, 32, 16, 8):
                    routes = routes + pltpu.roll(routes, by, 1)
                route_out[span, :] = routes
    for copy in sent:
        copy.wait_send()
    for copy in stores:
        copy.wait()


def finish(
    tile, route, mixed, d_tokens, xs, ds, hw, dg, du, route_out, mixed_out, dtok_out, gg, gu, gd,
    x_in, d_in, hw_in, dg_in, du_in, stage, load_sem, store_sem,
):
    def copy(source, target, sem):
        made = pltpu.make_async_copy(source, target, sem)
        made.start()
        return made

    moves = ((hw, hw_in), (ds, d_in), (dg, dg_in), (xs, x_in), (du, du_in))
    loads = [copy(source, target, load_sem.at[k]) for k, (source, target) in enumerate(moves)]
    stores = [copy(mixed, mixed_out, store_sem.at[0]), copy(d_tokens, dtok_out, store_sem.at[1])]
    route_out[...] = jnp.transpose(route[...])[: route_out.shape[0]]
    half = xs.shape[3]
    total_rows = hw.shape[1]
    for number, (left, buffer, target, ready) in enumerate(
        ((hw_in, d_in, gd, 2), (dg_in, x_in, gg, 2), (du_in, x_in, gu, 1))
    ):
        for _ in range(ready):
            loads.pop(0).wait()
        for part in range(CORES):

            @pl.loop(0, half // tile)
            def columns(t):
                right = buffer[part, :, :, pl.ds(pl.multiple_of(t * tile, tile), tile)]
                start = pl.multiple_of(part * half + t * tile, tile)
                stage[number, :, pl.ds(start, tile)] = dot(
                    left[...], right.reshape(total_rows, tile), 1, 0
                ).astype(BF16)

            span = pl.ds(part * half, half)
            stores.append(
                copy(
                    stage.at[number, :, span], target.at[0, :, span],
                    store_sem.at[2 + CORES * number + part],
                )
            )
    for store in stores:
        store.wait()


def body(tokens, d_mixed, route_ids, route_weight, gate_weight, up_weight, down_weight):
    n_dp = lax.axis_size("dp")
    n_z = lax.axis_size("expert") // CORES
    side = math.isqrt(n_dp)
    rows, width = tokens.shape
    choices = route_ids.shape[1]
    hid = gate_weight.shape[1]
    half = width // CORES
    tile = 256
    row_parts = min(n_z, rows // 16)
    col_parts = n_z // row_parts
    high = rows // row_parts
    chunks = ((0, half), (0, half // 2), (half // 2, half // 2))
    plain_widths = tuple(wide for _, wide in chunks)
    widths = (half, half // 2 + 128 * col_parts, half // 2)
    total_rows = n_dp * rows

    def vmem(*dims, dtype=BF16):
        return pltpu.VMEM(dims, dtype)

    def each(make, sizes=widths):
        return [make(w) for w in sizes]

    scratch = [vmem(CORES, n_dp, rows, half)] * 2
    scratch += [vmem(hid, width)] * 3
    scratch += [vmem(hid, total_rows, dtype=F32)] * 4
    scratch += [vmem(8, total_rows, dtype=jnp.int32), vmem(8, total_rows, dtype=F32)]
    scratch += [vmem(1, total_rows, dtype=F32)]
    scratch += [vmem(hid, total_rows)] * 3
    scratch += [vmem(total_rows, hid)] * 3
    scratch += each(lambda w: vmem(n_dp, rows, w), plain_widths) * 2
    scratch += each(lambda w: vmem(n_dp, rows, w, dtype=F32))
    scratch += each(lambda w: vmem(n_dp, rows, w))
    scratch += each(lambda w: vmem(side - 1, side, rows, w))
    scratch += each(lambda w: vmem(side - 1, rows, w))
    scratch += each(lambda w: vmem(side - 1, rows, w))
    scratch += each(lambda w: vmem(n_z, high, w // col_parts))
    scratch += each(lambda w: vmem(n_z, high, w // col_parts, dtype=F32))
    scratch += each(lambda w: vmem(n_z - 1, high, w // col_parts))
    scratch += each(lambda w: vmem(CORES, n_z, high, w // col_parts))
    gather = 2 * (2 * (side - 1) + (side - 1) ** 2 + n_dp - 1)
    reduce = len(chunks) * (1 + (side - 1) * side + side - 1 + 2 * (n_z - 1) + n_z)
    copies = gather + reduce
    scratch += [pltpu.SemaphoreType.DMA((copies,))] * 2
    scratch += [pltpu.SemaphoreType.DMA((3,)), pltpu.SemaphoreType.DMA((5,))]

    in_vmem = pl.BlockSpec(memory_space=pltpu.VMEM)
    anywhere = pl.BlockSpec(memory_space=pl.ANY)
    flat = jax.ShapeDtypeStruct((rows, width), BF16)
    gathered = jax.ShapeDtypeStruct((CORES, n_dp, rows, half), BF16)
    left = jax.ShapeDtypeStruct((hid, total_rows), BF16)
    shape = (n_dp, side, n_z, rows, half, row_parts, tile, chunks)
    results = pl.pallas_call(
        functools.partial(kernel, shape),
        out_shape=(flat, jax.ShapeDtypeStruct((rows, 128), F32), flat)
        + (gathered,) * 2 + (left,) * 3,
        in_specs=[in_vmem] * 4 + [anywhere] * 3,
        out_specs=(in_vmem,) * 3 + (anywhere,) * 5,
        scratch_shapes=scratch,
        compiler_params=pltpu.CompilerParams(
            collective_id=0, has_side_effects=True, vmem_limit_bytes=60 * 1024 * 1024
        ),
        cost_estimate=pl.CostEstimate(
            flops=12 * total_rows * hid * width,
            bytes_accessed=6 * hid * width,
            transcendentals=total_rows * hid,
        ),
    )(tokens, d_mixed, route_ids.T, route_weight.T, gate_weight, up_weight, down_weight)

    mixed, route, d_tokens, *operands = results
    grad = jax.ShapeDtypeStruct((1, hid, width), BF16)
    route, mixed, d_tokens, grad_gate, grad_up, grad_down = pl.pallas_call(
        functools.partial(finish, 2 * tile),
        out_shape=(jax.ShapeDtypeStruct((choices, rows), F32), flat, flat, grad, grad, grad),
        in_specs=[in_vmem] + [anywhere] * 7,
        out_specs=(in_vmem,) + (anywhere,) * 5,
        scratch_shapes=[vmem(CORES, n_dp, rows, half)] * 2
        + [vmem(hid, total_rows)] * 3
        + [vmem(3, hid, width), pltpu.SemaphoreType.DMA((5,)), pltpu.SemaphoreType.DMA((8,))],
        compiler_params=pltpu.CompilerParams(vmem_limit_bytes=60 * 1024 * 1024),
        cost_estimate=pl.CostEstimate(
            flops=6 * total_rows * hid * width,
            bytes_accessed=6 * hid * width,
            transcendentals=0,
        ),
    )(route, mixed, d_tokens, *operands)
    return mixed, route.T, d_tokens, grad_gate, grad_up, grad_down


def solution(mesh):
    row, whole, block = P("dp", None), P(), P(("expert", "dp"), None, None)
    return jax.shard_map(
        body,
        mesh=mesh,
        in_specs=(row, row, whole, whole, block, block, block),
        out_specs=(row, row, row, block, block, block),
        check_vma=False,
    )
```

```python
import functools

import jax
import jax.numpy as jnp
from jax import lax
from jax.experimental import pallas as pl
from jax.experimental.pallas import tpu as pltpu
from jax.sharding import PartitionSpec as P

EXP_DEV = 2
CORES = 2
MESH = pl.DeviceIdType.MESH
F32 = jnp.float32
BF16 = jnp.bfloat16


def dot(left, right, lhs_dim, rhs_dim):
    return lax.dot_general(
        left, right, (((lhs_dim,), (rhs_dim,)), ((), ())), preferred_element_type=F32
    )


def kernel(
    shape, tok, dmx, ids, wts, gate_hbm, up_hbm, down_hbm,
    mixed_out, route_out, dtok_out, xs_out, ds_out, hw_out, dg_out, du_out, *scratch,
):
    n_dp, n_z, rows, half, row_parts, tile, chunks = shape
    scratch = list(scratch)

    def take(count):
        taken = scratch[:count]
        del scratch[:count]
        return taken

    xs, ds, wg, wu, wd, gate, up, hidf, dhid, ids8, wts8, paired = take(12)
    turned = take(3)
    hw, dg, du = take(3)
    count = len(chunks)
    ps, pr, acc, sb, rb, zb, zf, rz, ag = [take(count) for _ in range(9)]
    send_sem, recv_sem, load_sem, store_sem = take(4)
    dp = lax.axis_index("dp")
    column = lax.axis_index("expert")
    core = lax.rem(column, CORES)
    z = column // CORES
    def turn(value, by, size):
        return lax.rem(value + by + size, size)

    sibling = (dp, column + 1 - 2 * core)

    def peer_dp(by):
        return (turn(dp, by, n_dp), column)

    def peer_z(by):
        return (dp, turn(z, by, n_z) * CORES + core)

    partners = [sibling]
    partners += [peer_dp(k) for k in range(1, n_dp)]
    partners += [peer_z(k) for k in range(1, n_z)]

    loads = []
    for number, (source, target) in enumerate(((gate_hbm, wg), (up_hbm, wu), (down_hbm, wd))):
        loads.append(pltpu.make_async_copy(source.at[0], target, load_sem.at[number]))
        loads[-1].start()

    used = [0]
    sent = []

    def send(source, target, device):
        copy = pltpu.make_async_remote_copy(
            src_ref=source, dst_ref=target, send_sem=send_sem.at[used[0]],
            recv_sem=recv_sem.at[used[0]], device_id=device, device_id_type=MESH,
        )
        used[0] += 1
        copy.start()
        sent.append(copy)
        return copy

    barrier = pltpu.get_barrier_semaphore()
    for partner in partners:
        pl.semaphore_signal(barrier, inc=1, device_id=partner, device_id_type=MESH)
    for part in range(CORES):
        xs[part, dp] = tok[:, part * half : (part + 1) * half]
        ds[part, dp] = dmx[:, part * half : (part + 1) * half]
    pl.semaphore_wait(barrier, len(partners))

    from_dp, from_core = [], [[], []]
    for buffer in (xs, ds):
        own = buffer.at[core, dp]
        from_dp.append([send(own, own, peer_dp(k)) for k in range(1, n_dp)])

    def pass_on(number, buffer):
        for k in range(1, n_dp):
            from_dp[number][k - 1].wait_recv()
            got = buffer.at[core, turn(dp, -k, n_dp)]
            from_core[number].append(send(got, got, sibling))

    def whole(buffer, part):
        return buffer[part].reshape(n_dp * rows, half)

    pieces = n_dp // EXP_DEV
    expert = column * EXP_DEV + dp // pieces
    piece = lax.rem(dp, pieces)
    choices = ids.shape[0]
    ids8[...] = jnp.full(ids8.shape, -1, jnp.int32)
    ids8[:choices, :] = ids[...]
    wts8[...] = jnp.zeros(wts8.shape, F32)
    wts8[:choices, :] = wts[...]
    named = ids8[...] == expert
    weight = jnp.sum(jnp.where(named, wts8[...], 0.0), axis=0, keepdims=True)

    stores = []

    def keep(source, target):
        stores.append(pltpu.make_async_copy(source, target, store_sem.at[len(stores)]))
        stores[-1].start()

    pass_on(0, xs)
    for copy in from_core[0]:
        copy.wait_recv()
    loads[0].wait()
    gate[...] = dot(wg[:, :half], whole(xs, 0), 1, 1) + dot(wg[:, half:], whole(xs, 1), 1, 1)
    loads[1].wait()
    up[...] = dot(wu[:, :half], whole(xs, 0), 1, 1) + dot(wu[:, half:], whole(xs, 1), 1, 1)
    hid = gate.shape[0]
    strip = 16 * max(k for k in range(1, 12) if hid // 16 % k == 0)

    @pl.loop(0, hid // strip)
    def forward(index):
        span = pl.ds(pl.multiple_of(index * strip, strip), strip)
        gate_value = gate[span, :]
        up_value = up[span, :]
        sigmoid_gate = 1.0 / (1.0 + jnp.exp(-gate_value))
        activated = gate_value * sigmoid_gate
        hidden = activated * up_value
        turned[0][span, :] = (weight * hidden).astype(BF16)
        hidf[span, :] = hidden
        up[span, :] = activated
        gate[span, :] = up_value * sigmoid_gate * (1.0 + gate_value * (1.0 - sigmoid_gate))

    hw[...] = jnp.transpose(turned[0][...])

    def product(q, columns):
        if q == 0:
            return dot(hw[...], wd[:, columns], 1, 0)
        return dot(dg[...], wg[:, columns], 1, 0) + dot(du[...], wu[:, columns], 1, 0)

    def other_half(q):
        first, wide = chunks[q]

        @pl.loop(0, wide // tile)
        def columns(t):
            start = pl.multiple_of((1 - core) * half + first + t * tile, tile)
            value = product(q, pl.ds(start, tile)).astype(BF16)
            ps[q][:, :, pl.ds(pl.multiple_of(t * tile, tile), tile)] = value.reshape(
                n_dp, rows, tile
            )

        return send(ps[q], pr[q], sibling)

    def own_half(q):
        first, wide = chunks[q]

        @pl.loop(0, wide // tile)
        def columns(t):
            start = pl.multiple_of(core * half + first + t * tile, tile)
            value = product(q, pl.ds(start, tile))
            acc[q][:, :, pl.ds(pl.multiple_of(t * tile, tile), tile)] = value.reshape(
                n_dp, rows, tile
            )

    def pair_done(q, copy):
        copy.wait_recv()
        wide = chunks[q][1]

        @pl.loop(0, n_dp)
        def add(block):
            total = acc[q][block, :, :wide] + pr[q][block].astype(F32)
            acc[q][block, :, :wide] = total
            sb[q][block, :, :wide] = total.astype(BF16)
            if acc[q].shape[2] > wide:
                sb[q][block, :, wide:] = acc[q][block, :, wide:].astype(BF16)

        return [
            send(sb[q].at[turn(dp, k, n_dp)], rb[q].at[k - 1], peer_dp(k)) for k in range(1, n_dp)
        ]

    def second_done(q, copies):
        for copy in copies:
            copy.wait_recv()
        total = acc[q][dp]
        for k in range(1, n_dp):
            total = total + rb[q][k - 1].astype(F32)
        high, wide = zb[q].shape[1:]
        for part in range(n_z):
            top = (part % row_parts) * high
            left = (part // row_parts) * wide
            value = total[top : top + high, left : left + wide]
            zf[q][part] = value
            zb[q][part] = value.astype(BF16)
        return [
            send(zb[q].at[turn(z, k, n_z)], rz[q].at[k - 1], peer_z(k)) for k in range(1, n_z)
        ]

    def third_done(q, copies):
        for copy in copies:
            copy.wait_recv()
        total = zf[q][z]
        for k in range(1, n_z):
            total = total + rz[q][k - 1].astype(F32)
        ag[q][core, z] = total.astype(BF16)
        own = ag[q].at[core, z]
        following = [send(own, own, peer_z(k)) for k in range(1, n_z)]
        shared = [send(own, own, sibling)]
        if q > 0:
            for k in range(1, n_z):
                other = turn(z, k, n_z) * CORES + 1 - core
                shared.append(send(own, own, (dp, other)))
            shared += following
        return following, shared

    def fourth_done(q, copies, shared):
        for k in range(1, n_z):
            copies[k - 1].wait_recv()
            got = ag[q].at[core, turn(z, -k, n_z)]
            shared.append(send(got, got, sibling))

    loads[2].wait()
    pair0 = other_half(0)
    pass_on(1, ds)
    own_half(0)
    step0 = pair_done(0, pair0)
    for copy in from_core[1]:
        copy.wait_recv()
    dhid[...] = dot(wd[:, :half], whole(ds, 0), 1, 1) + dot(wd[:, half:], whole(ds, 1), 1, 1)
    paired[...] = jnp.zeros(paired.shape, F32)

    @pl.loop(0, hid // strip)
    def backward(index):
        span = pl.ds(pl.multiple_of(index * strip, strip), strip)
        plain = dhid[span, :]
        paired[...] += jnp.sum(hidf[span, :] * plain, axis=0, keepdims=True)
        d_hidden = weight * plain
        turned[1][span, :] = (d_hidden * gate[span, :]).astype(BF16)
        turned[2][span, :] = (d_hidden * up[span, :]).astype(BF16)

    dg[...] = jnp.transpose(turned[1][...])
    du[...] = jnp.transpose(turned[2][...])
    share = paired[...]
    leading = share.astype(BF16).astype(F32)
    kept = jnp.where(named, leading, 0.0)
    rest = jnp.where(named, share - leading, 0.0)
    groups = [jnp.where(piece == k, kept, 0.0) for k in range(8)]
    groups += [jnp.where(piece == k, rest, 0.0) for k in range(8)]
    lanes = jnp.transpose(jnp.concatenate(groups, axis=0)).reshape(n_dp, rows, 128)
    wide = chunks[1][1]
    acc[1][:, :, wide : wide + 128] = lanes
    extra = acc[1].shape[2] - wide - 128
    if extra:
        acc[1][:, :, wide + 128 :] = jnp.zeros((n_dp, rows, extra), F32)

    pair1 = other_half(1)
    own_half(1)
    step1 = pair_done(1, pair1)
    pair2 = other_half(2)
    step0 = second_done(0, step0)
    own_half(2)
    step2 = pair_done(2, pair2)
    step1 = second_done(1, step1)
    keep(xs, xs_out)
    keep(ds, ds_out)
    for source, target in zip(turned, (hw_out, dg_out, du_out)):
        keep(source, target)
    step0, shared0 = third_done(0, step0)
    step2 = second_done(2, step2)
    unused, shared1 = third_done(1, step1)
    fourth_done(0, step0, shared0)
    unused, shared2 = third_done(2, step2)

    for q, (target, shared) in enumerate(
        ((mixed_out, shared0), (dtok_out, shared1), (dtok_out, shared2))
    ):
        for copy in shared:
            copy.wait_recv()
        first, width = chunks[q]
        high = zb[q].shape[1]
        for part in range(row_parts):
            span = slice(part * high, (part + 1) * high)
            routes = 0.0
            for side_core in range(CORES):
                strips = [ag[q][side_core, k * row_parts + part] for k in range(n_z // row_parts)]
                line = strips[0] if len(strips) == 1 else jnp.concatenate(strips, axis=1)
                left = side_core * half + first
                target[span, left : left + width] = line[:, :width]
                if q == 1:
                    routes = routes + line[:, width : width + 128].astype(F32)
            if q == 1:
                for by in (64, 32, 16, 8):
                    routes = routes + pltpu.roll(routes, by, 1)
                route_out[span, :] = routes
    for copy in sent:
        copy.wait_send()
    for copy in stores:
        copy.wait()


def finish(
    tile, route, mixed, d_tokens, xs, ds, hw, dg, du, route_out, mixed_out, dtok_out, gg, gu, gd,
    x_in, d_in, hw_in, dg_in, du_in, m_in, t_in, stage, load_sem, store_sem,
):
    def copy(source, target, sem):
        made = pltpu.make_async_copy(source, target, sem)
        made.start()
        return made

    moves = (
        (hw, hw_in), (ds, d_in), (mixed, m_in), (d_tokens, t_in), (dg, dg_in), (xs, x_in), (du, du_in)
    )
    loads = [copy(source, target, load_sem.at[k]) for k, (source, target) in enumerate(moves)]
    stores = []
    route_out[...] = jnp.transpose(route[...])[: route_out.shape[0]]
    half = xs.shape[3]
    total_rows = hw.shape[1]
    for number, (left, buffer, target, ready) in enumerate(
        ((hw_in, d_in, gd, 2), (dg_in, x_in, gg, 4), (du_in, x_in, gu, 1))
    ):
        for _ in range(ready):
            loads.pop(0).wait()
        if number == 1:
            stores.append(copy(m_in, mixed_out, store_sem.at[0]))
            stores.append(copy(t_in, dtok_out, store_sem.at[1]))
        for part in range(CORES):

            @pl.loop(0, half // tile)
            def columns(t):
                right = buffer[part, :, :, pl.ds(pl.multiple_of(t * tile, tile), tile)]
                start = pl.multiple_of(part * half + t * tile, tile)
                stage[number, :, pl.ds(start, tile)] = dot(
                    left[...], right.reshape(total_rows, tile), 1, 0
                ).astype(BF16)

            span = pl.ds(part * half, half)
            stores.append(
                copy(
                    stage.at[number, :, span], target.at[0, :, span],
                    store_sem.at[2 + CORES * number + part],
                )
            )
    for store in stores:
        store.wait()


def body(tokens, d_mixed, route_ids, route_weight, gate_weight, up_weight, down_weight):
    n_dp = lax.axis_size("dp")
    n_z = lax.axis_size("expert") // CORES
    rows, width = tokens.shape
    choices = route_ids.shape[1]
    hid = gate_weight.shape[1]
    half = width // CORES
    tile = 256
    row_parts = min(n_z, rows // 16)
    col_parts = n_z // row_parts
    high = rows // row_parts
    chunks = ((0, half), (0, half // 2), (half // 2, half // 2))
    plain_widths = tuple(wide for _, wide in chunks)
    widths = (half, half // 2 + 128 * col_parts, half // 2)
    total_rows = n_dp * rows

    def vmem(*dims, dtype=BF16):
        return pltpu.VMEM(dims, dtype)

    def each(make, sizes=widths):
        return [make(w) for w in sizes]

    scratch = [vmem(CORES, n_dp, rows, half)] * 2
    scratch += [vmem(hid, width)] * 3
    scratch += [vmem(hid, total_rows, dtype=F32)] * 4
    scratch += [vmem(8, total_rows, dtype=jnp.int32), vmem(8, total_rows, dtype=F32)]
    scratch += [vmem(1, total_rows, dtype=F32)]
    scratch += [vmem(hid, total_rows)] * 3
    scratch += [vmem(total_rows, hid)] * 3
    scratch += each(lambda w: vmem(n_dp, rows, w), plain_widths) * 2
    scratch += each(lambda w: vmem(n_dp, rows, w, dtype=F32))
    scratch += each(lambda w: vmem(n_dp, rows, w))
    scratch += each(lambda w: vmem(n_dp - 1, rows, w))
    scratch += each(lambda w: vmem(n_z, high, w // col_parts))
    scratch += each(lambda w: vmem(n_z, high, w // col_parts, dtype=F32))
    scratch += each(lambda w: vmem(n_z - 1, high, w // col_parts))
    scratch += each(lambda w: vmem(CORES, n_z, high, w // col_parts))
    gather = 4 * (n_dp - 1)
    reduce = len(chunks) * (n_dp + 3 * n_z - 2)
    copies = gather + reduce
    scratch += [pltpu.SemaphoreType.DMA((copies,))] * 2
    scratch += [pltpu.SemaphoreType.DMA((3,)), pltpu.SemaphoreType.DMA((5,))]

    in_vmem = pl.BlockSpec(memory_space=pltpu.VMEM)
    anywhere = pl.BlockSpec(memory_space=pl.ANY)
    flat = jax.ShapeDtypeStruct((rows, width), BF16)
    gathered = jax.ShapeDtypeStruct((CORES, n_dp, rows, half), BF16)
    left = jax.ShapeDtypeStruct((hid, total_rows), BF16)
    shape = (n_dp, n_z, rows, half, row_parts, tile, chunks)
    results = pl.pallas_call(
        functools.partial(kernel, shape),
        out_shape=(flat, jax.ShapeDtypeStruct((rows, 128), F32), flat)
        + (gathered,) * 2 + (left,) * 3,
        in_specs=[in_vmem] * 4 + [anywhere] * 3,
        out_specs=(in_vmem,) * 3 + (anywhere,) * 5,
        scratch_shapes=scratch,
        compiler_params=pltpu.CompilerParams(
            collective_id=0, has_side_effects=True, vmem_limit_bytes=60 * 1024 * 1024
        ),
        cost_estimate=pl.CostEstimate(
            flops=12 * total_rows * hid * width,
            bytes_accessed=6 * hid * width,
            transcendentals=total_rows * hid,
        ),
    )(tokens, d_mixed, route_ids.T, route_weight.T, gate_weight, up_weight, down_weight)

    mixed, route, d_tokens, *operands = results
    grad = jax.ShapeDtypeStruct((1, hid, width), BF16)
    route, mixed, d_tokens, grad_gate, grad_up, grad_down = pl.pallas_call(
        functools.partial(finish, 2 * tile),
        out_shape=(jax.ShapeDtypeStruct((choices, rows), F32), flat, flat, grad, grad, grad),
        in_specs=[in_vmem] + [anywhere] * 7,
        out_specs=(in_vmem,) + (anywhere,) * 5,
        scratch_shapes=[vmem(CORES, n_dp, rows, half)] * 2
        + [vmem(hid, total_rows)] * 3
        + [vmem(rows, width)] * 2
        + [vmem(3, hid, width), pltpu.SemaphoreType.DMA((7,)), pltpu.SemaphoreType.DMA((8,))],
        compiler_params=pltpu.CompilerParams(vmem_limit_bytes=60 * 1024 * 1024),
        cost_estimate=pl.CostEstimate(
            flops=6 * total_rows * hid * width,
            bytes_accessed=6 * hid * width,
            transcendentals=0,
        ),
    )(route, mixed, d_tokens, *operands)
    return mixed, route.T, d_tokens, grad_gate, grad_up, grad_down


def solution(mesh):
    row, whole, block = P("dp", None), P(), P(("expert", "dp"), None, None)
    return jax.shard_map(
        body,
        mesh=mesh,
        in_specs=(row, row, whole, whole, block, block, block),
        out_specs=(row, row, row, block, block, block),
        check_vma=False,
    )
```

```python
import functools

import jax
import jax.numpy as jnp
from jax import lax
from jax.experimental import pallas as pl
from jax.experimental.pallas import tpu as pltpu
from jax.sharding import PartitionSpec as P

EXP_DEV = 2
CORES = 2
MESH = pl.DeviceIdType.MESH
F32 = jnp.float32
BF16 = jnp.bfloat16


def dot(left, right, lhs_dim, rhs_dim):
    return lax.dot_general(
        left, right, (((lhs_dim,), (rhs_dim,)), ((), ())), preferred_element_type=F32
    )


def kernel(
    shape, tok, dmx, ids, wts, gate_hbm, up_hbm, down_hbm,
    mixed_out, route_out, dtok_out, xs_out, ds_out, hw_out, dg_out, du_out, *scratch,
):
    n_dp, n_z, rows, half, row_parts, tile, chunks = shape
    scratch = list(scratch)

    def take(count):
        taken = scratch[:count]
        del scratch[:count]
        return taken

    xs, ds, wg, wu, wd, gate, up, hidf, dhid, ids8, wts8, paired = take(12)
    turned = take(3)
    hw, dg, du = take(3)
    count = len(chunks)
    ps, pr, acc, sb, rb, zb, zf, rz, ag = [take(count) for _ in range(9)]
    send_sem, recv_sem, load_sem, store_sem = take(4)
    dp = lax.axis_index("dp")
    column = lax.axis_index("expert")
    core = lax.rem(column, CORES)
    z = column // CORES
    def turn(value, by, size):
        return lax.rem(value + by + size, size)

    sibling = (dp, column + 1 - 2 * core)

    def peer_dp(by):
        return (turn(dp, by, n_dp), column)

    def peer_z(by):
        return (dp, turn(z, by, n_z) * CORES + core)

    partners = [sibling]
    partners += [peer_dp(k) for k in range(1, n_dp)]
    partners += [peer_z(k) for k in range(1, n_z)]

    loads = []
    for number, (source, target) in enumerate(((gate_hbm, wg), (up_hbm, wu), (down_hbm, wd))):
        loads.append(pltpu.make_async_copy(source.at[0], target, load_sem.at[number]))
        loads[-1].start()

    used = [0]
    sent = []

    def send(source, target, device):
        copy = pltpu.make_async_remote_copy(
            src_ref=source, dst_ref=target, send_sem=send_sem.at[used[0]],
            recv_sem=recv_sem.at[used[0]], device_id=device, device_id_type=MESH,
        )
        used[0] += 1
        copy.start()
        sent.append(copy)
        return copy

    barrier = pltpu.get_barrier_semaphore()
    for partner in partners:
        pl.semaphore_signal(barrier, inc=1, device_id=partner, device_id_type=MESH)
    for part in range(CORES):
        xs[part, dp] = tok[:, part * half : (part + 1) * half]
        ds[part, dp] = dmx[:, part * half : (part + 1) * half]
    pl.semaphore_wait(barrier, len(partners))

    from_dp, from_core = [], [[], []]
    for buffer in (xs, ds):
        own = buffer.at[core, dp]
        from_dp.append([send(own, own, peer_dp(k)) for k in range(1, n_dp)])

    def pass_on(number, buffer):
        for k in range(1, n_dp):
            from_dp[number][k - 1].wait_recv()
            got = buffer.at[core, turn(dp, -k, n_dp)]
            from_core[number].append(send(got, got, sibling))

    def whole(buffer, part):
        return buffer[part].reshape(n_dp * rows, half)

    pieces = n_dp // EXP_DEV
    expert = column * EXP_DEV + dp // pieces
    piece = lax.rem(dp, pieces)
    choices = ids.shape[0]
    ids8[...] = jnp.full(ids8.shape, -1, jnp.int32)
    ids8[:choices, :] = ids[...]
    wts8[...] = jnp.zeros(wts8.shape, F32)
    wts8[:choices, :] = wts[...]
    named = ids8[...] == expert
    weight = jnp.sum(jnp.where(named, wts8[...], 0.0), axis=0, keepdims=True)

    stores = []

    def keep(source, target):
        stores.append(pltpu.make_async_copy(source, target, store_sem.at[len(stores)]))
        stores[-1].start()

    pass_on(0, xs)
    for copy in from_core[0]:
        copy.wait_recv()
    loads[0].wait()
    gate[...] = dot(wg[:, :half], whole(xs, 0), 1, 1) + dot(wg[:, half:], whole(xs, 1), 1, 1)
    loads[1].wait()
    up[...] = dot(wu[:, :half], whole(xs, 0), 1, 1) + dot(wu[:, half:], whole(xs, 1), 1, 1)
    hid = gate.shape[0]
    strip = 16 * max(k for k in range(1, 12) if hid // 16 % k == 0)

    @pl.loop(0, hid // strip)
    def forward(index):
        span = pl.ds(pl.multiple_of(index * strip, strip), strip)
        gate_value = gate[span, :]
        up_value = up[span, :]
        sigmoid_gate = 1.0 / (1.0 + jnp.exp(-gate_value))
        activated = gate_value * sigmoid_gate
        hidden = activated * up_value
        turned[0][span, :] = (weight * hidden).astype(BF16)
        hidf[span, :] = hidden
        up[span, :] = activated
        gate[span, :] = up_value * sigmoid_gate * (1.0 + gate_value * (1.0 - sigmoid_gate))

    hw[...] = jnp.transpose(turned[0][...])

    def product(q, columns):
        if q == 0:
            return dot(hw[...], wd[:, columns], 1, 0)
        return dot(dg[...], wg[:, columns], 1, 0) + dot(du[...], wu[:, columns], 1, 0)

    def other_half(q):
        first, wide = chunks[q]

        @pl.loop(0, wide // tile)
        def columns(t):
            start = pl.multiple_of((1 - core) * half + first + t * tile, tile)
            value = product(q, pl.ds(start, tile)).astype(BF16)
            ps[q][:, :, pl.ds(pl.multiple_of(t * tile, tile), tile)] = value.reshape(
                n_dp, rows, tile
            )

        return send(ps[q], pr[q], sibling)

    def own_half(q):
        first, wide = chunks[q]

        @pl.loop(0, wide // tile)
        def columns(t):
            start = pl.multiple_of(core * half + first + t * tile, tile)
            value = product(q, pl.ds(start, tile))
            acc[q][:, :, pl.ds(pl.multiple_of(t * tile, tile), tile)] = value.reshape(
                n_dp, rows, tile
            )

    def pair_done(q, copy):
        copy.wait_recv()
        wide = chunks[q][1]

        @pl.loop(0, n_dp)
        def add(block):
            total = acc[q][block, :, :wide] + pr[q][block].astype(F32)
            acc[q][block, :, :wide] = total
            sb[q][block, :, :wide] = total.astype(BF16)
            if acc[q].shape[2] > wide:
                sb[q][block, :, wide:] = acc[q][block, :, wide:].astype(BF16)

        return [
            send(sb[q].at[turn(dp, k, n_dp)], rb[q].at[k - 1], peer_dp(k)) for k in range(1, n_dp)
        ]

    def second_done(q, copies):
        for copy in copies:
            copy.wait_recv()
        total = acc[q][dp]
        for k in range(1, n_dp):
            total = total + rb[q][k - 1].astype(F32)
        high, wide = zb[q].shape[1:]
        for part in range(n_z):
            top = (part % row_parts) * high
            left = (part // row_parts) * wide
            value = total[top : top + high, left : left + wide]
            zf[q][part] = value
            zb[q][part] = value.astype(BF16)
        return [
            send(zb[q].at[turn(z, k, n_z)], rz[q].at[k - 1], peer_z(k)) for k in range(1, n_z)
        ]

    def third_done(q, copies):
        for copy in copies:
            copy.wait_recv()
        total = zf[q][z]
        for k in range(1, n_z):
            total = total + rz[q][k - 1].astype(F32)
        ag[q][core, z] = total.astype(BF16)
        own = ag[q].at[core, z]
        following = [send(own, own, peer_z(k)) for k in range(1, n_z)]
        shared = [send(own, own, sibling)]
        return following, shared

    def fourth_done(q, copies, shared):
        for k in range(1, n_z):
            copies[k - 1].wait_recv()
            got = ag[q].at[core, turn(z, -k, n_z)]
            shared.append(send(got, got, sibling))

    loads[2].wait()
    pair0 = other_half(0)
    pass_on(1, ds)
    own_half(0)
    step0 = pair_done(0, pair0)
    for copy in from_core[1]:
        copy.wait_recv()
    dhid[...] = dot(wd[:, :half], whole(ds, 0), 1, 1) + dot(wd[:, half:], whole(ds, 1), 1, 1)
    paired[...] = jnp.zeros(paired.shape, F32)

    @pl.loop(0, hid // strip)
    def backward(index):
        span = pl.ds(pl.multiple_of(index * strip, strip), strip)
        plain = dhid[span, :]
        paired[...] += jnp.sum(hidf[span, :] * plain, axis=0, keepdims=True)
        d_hidden = weight * plain
        turned[1][span, :] = (d_hidden * gate[span, :]).astype(BF16)
        turned[2][span, :] = (d_hidden * up[span, :]).astype(BF16)

    dg[...] = jnp.transpose(turned[1][...])
    du[...] = jnp.transpose(turned[2][...])
    share = paired[...]
    leading = share.astype(BF16).astype(F32)
    kept = jnp.where(named, leading, 0.0)
    rest = jnp.where(named, share - leading, 0.0)
    groups = [jnp.where(piece == k, kept, 0.0) for k in range(8)]
    groups += [jnp.where(piece == k, rest, 0.0) for k in range(8)]
    lanes = jnp.transpose(jnp.concatenate(groups, axis=0)).reshape(n_dp, rows, 128)
    wide = chunks[1][1]
    acc[1][:, :, wide : wide + 128] = lanes
    extra = acc[1].shape[2] - wide - 128
    if extra:
        acc[1][:, :, wide + 128 :] = jnp.zeros((n_dp, rows, extra), F32)

    pair1 = other_half(1)
    own_half(1)
    step1 = pair_done(1, pair1)
    pair2 = other_half(2)
    step0 = second_done(0, step0)
    own_half(2)
    step2 = pair_done(2, pair2)
    step1 = second_done(1, step1)
    keep(xs, xs_out)
    keep(ds, ds_out)
    for source, target in zip(turned, (hw_out, dg_out, du_out)):
        keep(source, target)
    step0, shared0 = third_done(0, step0)
    step2 = second_done(2, step2)
    step1, shared1 = third_done(1, step1)
    fourth_done(0, step0, shared0)
    step2, shared2 = third_done(2, step2)
    fourth_done(1, step1, shared1)
    fourth_done(2, step2, shared2)

    for q, (target, shared) in enumerate(
        ((mixed_out, shared0), (dtok_out, shared1), (dtok_out, shared2))
    ):
        for copy in shared:
            copy.wait_recv()
        first, width = chunks[q]
        high = zb[q].shape[1]
        for part in range(row_parts):
            span = slice(part * high, (part + 1) * high)
            routes = 0.0
            for side_core in range(CORES):
                strips = [ag[q][side_core, k * row_parts + part] for k in range(n_z // row_parts)]
                line = strips[0] if len(strips) == 1 else jnp.concatenate(strips, axis=1)
                left = side_core * half + first
                target[span, left : left + width] = line[:, :width]
                if q == 1:
                    routes = routes + line[:, width : width + 128].astype(F32)
            if q == 1:
                for by in (64, 32, 16, 8):
                    routes = routes + pltpu.roll(routes, by, 1)
                route_out[span, :] = routes
    for copy in sent:
        copy.wait_send()
    for copy in stores:
        copy.wait()


def finish(
    tile, route, mixed, d_tokens, xs, ds, hw, dg, du, route_out, mixed_out, dtok_out, gg, gu, gd,
    x_in, d_in, hw_in, dg_in, du_in, m_in, t_in, stage, load_sem, store_sem,
):
    def copy(source, target, sem):
        made = pltpu.make_async_copy(source, target, sem)
        made.start()
        return made

    moves = (
        (hw, hw_in), (ds, d_in), (mixed, m_in), (d_tokens, t_in), (dg, dg_in), (xs, x_in), (du, du_in)
    )
    loads = [copy(source, target, load_sem.at[k]) for k, (source, target) in enumerate(moves)]
    stores = []
    route_out[...] = jnp.transpose(route[...])[: route_out.shape[0]]
    half = xs.shape[3]
    total_rows = hw.shape[1]
    for number, (left, buffer, target, ready) in enumerate(
        ((hw_in, d_in, gd, 2), (dg_in, x_in, gg, 4), (du_in, x_in, gu, 1))
    ):
        for _ in range(ready):
            loads.pop(0).wait()
        if number == 1:
            stores.append(copy(m_in, mixed_out, store_sem.at[0]))
            stores.append(copy(t_in, dtok_out, store_sem.at[1]))
        for part in range(CORES):

            @pl.loop(0, half // tile)
            def columns(t):
                right = buffer[part, :, :, pl.ds(pl.multiple_of(t * tile, tile), tile)]
                start = pl.multiple_of(part * half + t * tile, tile)
                stage[number, :, pl.ds(start, tile)] = dot(
                    left[...], right.reshape(total_rows, tile), 1, 0
                ).astype(BF16)

            span = pl.ds(part * half, half)
            stores.append(
                copy(
                    stage.at[number, :, span], target.at[0, :, span],
                    store_sem.at[2 + CORES * number + part],
                )
            )
    for store in stores:
        store.wait()


def body(tokens, d_mixed, route_ids, route_weight, gate_weight, up_weight, down_weight):
    n_dp = lax.axis_size("dp")
    n_z = lax.axis_size("expert") // CORES
    rows, width = tokens.shape
    choices = route_ids.shape[1]
    hid = gate_weight.shape[1]
    half = width // CORES
    tile = 256
    row_parts = min(n_z, rows // 16)
    col_parts = n_z // row_parts
    high = rows // row_parts
    chunks = ((0, half), (0, half // 2), (half // 2, half // 2))
    plain_widths = tuple(wide for _, wide in chunks)
    widths = (half, half // 2 + 128 * col_parts, half // 2)
    total_rows = n_dp * rows

    def vmem(*dims, dtype=BF16):
        return pltpu.VMEM(dims, dtype)

    def each(make, sizes=widths):
        return [make(w) for w in sizes]

    scratch = [vmem(CORES, n_dp, rows, half)] * 2
    scratch += [vmem(hid, width)] * 3
    scratch += [vmem(hid, total_rows, dtype=F32)] * 4
    scratch += [vmem(8, total_rows, dtype=jnp.int32), vmem(8, total_rows, dtype=F32)]
    scratch += [vmem(1, total_rows, dtype=F32)]
    scratch += [vmem(hid, total_rows)] * 3
    scratch += [vmem(total_rows, hid)] * 3
    scratch += each(lambda w: vmem(n_dp, rows, w), plain_widths) * 2
    scratch += each(lambda w: vmem(n_dp, rows, w, dtype=F32))
    scratch += each(lambda w: vmem(n_dp, rows, w))
    scratch += each(lambda w: vmem(n_dp - 1, rows, w))
    scratch += each(lambda w: vmem(n_z, high, w // col_parts))
    scratch += each(lambda w: vmem(n_z, high, w // col_parts, dtype=F32))
    scratch += each(lambda w: vmem(n_z - 1, high, w // col_parts))
    scratch += each(lambda w: vmem(CORES, n_z, high, w // col_parts))
    gather = 4 * (n_dp - 1)
    reduce = len(chunks) * (n_dp + 3 * n_z - 2)
    copies = gather + reduce
    scratch += [pltpu.SemaphoreType.DMA((copies,))] * 2
    scratch += [pltpu.SemaphoreType.DMA((3,)), pltpu.SemaphoreType.DMA((5,))]

    in_vmem = pl.BlockSpec(memory_space=pltpu.VMEM)
    anywhere = pl.BlockSpec(memory_space=pl.ANY)
    flat = jax.ShapeDtypeStruct((rows, width), BF16)
    gathered = jax.ShapeDtypeStruct((CORES, n_dp, rows, half), BF16)
    left = jax.ShapeDtypeStruct((hid, total_rows), BF16)
    shape = (n_dp, n_z, rows, half, row_parts, tile, chunks)
    results = pl.pallas_call(
        functools.partial(kernel, shape),
        out_shape=(flat, jax.ShapeDtypeStruct((rows, 128), F32), flat)
        + (gathered,) * 2 + (left,) * 3,
        in_specs=[in_vmem] * 4 + [anywhere] * 3,
        out_specs=(in_vmem,) * 3 + (anywhere,) * 5,
        scratch_shapes=scratch,
        compiler_params=pltpu.CompilerParams(
            collective_id=0, has_side_effects=True, vmem_limit_bytes=60 * 1024 * 1024
        ),
        cost_estimate=pl.CostEstimate(
            flops=12 * total_rows * hid * width,
            bytes_accessed=6 * hid * width,
            transcendentals=total_rows * hid,
        ),
    )(tokens, d_mixed, route_ids.T, route_weight.T, gate_weight, up_weight, down_weight)

    mixed, route, d_tokens, *operands = results
    grad = jax.ShapeDtypeStruct((1, hid, width), BF16)
    route, mixed, d_tokens, grad_gate, grad_up, grad_down = pl.pallas_call(
        functools.partial(finish, 2 * tile),
        out_shape=(jax.ShapeDtypeStruct((choices, rows), F32), flat, flat, grad, grad, grad),
        in_specs=[in_vmem] + [anywhere] * 7,
        out_specs=(in_vmem,) + (anywhere,) * 5,
        scratch_shapes=[vmem(CORES, n_dp, rows, half)] * 2
        + [vmem(hid, total_rows)] * 3
        + [vmem(rows, width)] * 2
        + [vmem(3, hid, width), pltpu.SemaphoreType.DMA((7,)), pltpu.SemaphoreType.DMA((8,))],
        compiler_params=pltpu.CompilerParams(vmem_limit_bytes=60 * 1024 * 1024),
        cost_estimate=pl.CostEstimate(
            flops=6 * total_rows * hid * width,
            bytes_accessed=6 * hid * width,
            transcendentals=0,
        ),
    )(route, mixed, d_tokens, *operands)
    return mixed, route.T, d_tokens, grad_gate, grad_up, grad_down


def solution(mesh):
    row, whole, block = P("dp", None), P(), P(("expert", "dp"), None, None)
    return jax.shard_map(
        body,
        mesh=mesh,
        in_specs=(row, row, whole, whole, block, block, block),
        out_specs=(row, row, row, block, block, block),
        check_vma=False,
    )
```

```python
import functools

import jax
import jax.numpy as jnp
from jax import lax
from jax.experimental import pallas as pl
from jax.experimental.pallas import tpu as pltpu
from jax.sharding import PartitionSpec as P

EXP_DEV = 2
CORES = 2
MESH = pl.DeviceIdType.MESH
F32 = jnp.float32
BF16 = jnp.bfloat16


def dot(left, right, lhs_dim, rhs_dim):
    return lax.dot_general(
        left, right, (((lhs_dim,), (rhs_dim,)), ((), ())), preferred_element_type=F32
    )


def kernel(
    shape, tok, dmx, ids, wts, gate_hbm, up_hbm, down_hbm,
    mixed_out, route_out, dtok_out, xs_out, ds_out, hw_out, dg_out, du_out, *scratch,
):
    n_dp, n_z, rows, half, row_parts, tile, chunks = shape
    scratch = list(scratch)

    def take(count):
        taken = scratch[:count]
        del scratch[:count]
        return taken

    xs, ds, wg, wu, wd, gate, up, hidf, dhid, ids8, wts8, paired = take(12)
    turned = take(3)
    hw, dg, du = take(3)
    count = len(chunks)
    ps, pr, acc, sb, rb, zb, zf, rz, ag = [take(count) for _ in range(9)]
    send_sem, recv_sem, load_sem, store_sem = take(4)
    dp = lax.axis_index("dp")
    column = lax.axis_index("expert")
    core = lax.rem(column, CORES)
    z = column // CORES
    def turn(value, by, size):
        return lax.rem(value + by + size, size)

    sibling = (dp, column + 1 - 2 * core)

    def peer_dp(by):
        return (turn(dp, by, n_dp), column)

    def peer_z(by):
        return (dp, turn(z, by, n_z) * CORES + core)

    partners = [sibling]
    partners += [peer_dp(k) for k in range(1, n_dp)]
    partners += [peer_z(k) for k in range(1, n_z)]

    loads = []
    for number, (source, target) in enumerate(((gate_hbm, wg), (up_hbm, wu), (down_hbm, wd))):
        loads.append(pltpu.make_async_copy(source.at[0], target, load_sem.at[number]))
        loads[-1].start()

    used = [0]
    sent = []

    def send(source, target, device):
        copy = pltpu.make_async_remote_copy(
            src_ref=source, dst_ref=target, send_sem=send_sem.at[used[0]],
            recv_sem=recv_sem.at[used[0]], device_id=device, device_id_type=MESH,
        )
        used[0] += 1
        copy.start()
        sent.append(copy)
        return copy

    barrier = pltpu.get_barrier_semaphore()
    for partner in partners:
        pl.semaphore_signal(barrier, inc=1, device_id=partner, device_id_type=MESH)
    for part in range(CORES):
        xs[part, dp] = tok[:, part * half : (part + 1) * half]
        ds[part, dp] = dmx[:, part * half : (part + 1) * half]
    pl.semaphore_wait(barrier, len(partners))

    from_dp, from_core = [], [[], []]
    for buffer in (xs, ds):
        own = buffer.at[core, dp]
        from_dp.append([send(own, own, peer_dp(k)) for k in range(1, n_dp)])

    def pass_on(number, buffer):
        for k in range(1, n_dp):
            from_dp[number][k - 1].wait_recv()
            got = buffer.at[core, turn(dp, -k, n_dp)]
            from_core[number].append(send(got, got, sibling))

    def whole(buffer, part):
        return buffer[part].reshape(n_dp * rows, half)

    pieces = n_dp // EXP_DEV
    expert = column * EXP_DEV + dp // pieces
    piece = lax.rem(dp, pieces)
    choices = ids.shape[0]
    ids8[...] = jnp.full(ids8.shape, -1, jnp.int32)
    ids8[:choices, :] = ids[...]
    wts8[...] = jnp.zeros(wts8.shape, F32)
    wts8[:choices, :] = wts[...]
    named = ids8[...] == expert
    weight = jnp.sum(jnp.where(named, wts8[...], 0.0), axis=0, keepdims=True)

    stores = []

    def keep(source, target):
        stores.append(pltpu.make_async_copy(source, target, store_sem.at[len(stores)]))
        stores[-1].start()

    pass_on(0, xs)
    for copy in from_core[0]:
        copy.wait_recv()
    loads[0].wait()
    gate[...] = dot(wg[:, :half], whole(xs, 0), 1, 1) + dot(wg[:, half:], whole(xs, 1), 1, 1)
    loads[1].wait()
    up[...] = dot(wu[:, :half], whole(xs, 0), 1, 1) + dot(wu[:, half:], whole(xs, 1), 1, 1)
    hid = gate.shape[0]
    strip = 16 * max(k for k in range(1, 12) if hid // 16 % k == 0)

    @pl.loop(0, hid // strip)
    def forward(index):
        span = pl.ds(pl.multiple_of(index * strip, strip), strip)
        gate_value = gate[span, :]
        up_value = up[span, :]
        sigmoid_gate = 1.0 / (1.0 + jnp.exp(-gate_value))
        activated = gate_value * sigmoid_gate
        hidden = activated * up_value
        turned[0][span, :] = (weight * hidden).astype(BF16)
        hidf[span, :] = hidden
        up[span, :] = activated
        gate[span, :] = up_value * sigmoid_gate * (1.0 + gate_value * (1.0 - sigmoid_gate))

    hw[...] = jnp.transpose(turned[0][...])

    def product(q, columns):
        if q == 0:
            return dot(hw[...], wd[:, columns], 1, 0)
        return dot(dg[...], wg[:, columns], 1, 0) + dot(du[...], wu[:, columns], 1, 0)

    def other_half(q):
        first, wide = chunks[q]

        @pl.loop(0, wide // tile)
        def columns(t):
            start = pl.multiple_of((1 - core) * half + first + t * tile, tile)
            value = product(q, pl.ds(start, tile)).astype(BF16)
            ps[q][:, :, pl.ds(pl.multiple_of(t * tile, tile), tile)] = value.reshape(
                n_dp, rows, tile
            )

        return send(ps[q], pr[q], sibling)

    def own_half(q):
        first, wide = chunks[q]

        @pl.loop(0, wide // tile)
        def columns(t):
            start = pl.multiple_of(core * half + first + t * tile, tile)
            value = product(q, pl.ds(start, tile))
            acc[q][:, :, pl.ds(pl.multiple_of(t * tile, tile), tile)] = value.reshape(
                n_dp, rows, tile
            )

    def pair_done(q, copy):
        copy.wait_recv()
        wide = chunks[q][1]

        @pl.loop(0, n_dp)
        def add(block):
            total = acc[q][block, :, :wide] + pr[q][block].astype(F32)
            acc[q][block, :, :wide] = total
            sb[q][block, :, :wide] = total.astype(BF16)
            if acc[q].shape[2] > wide:
                sb[q][block, :, wide:] = acc[q][block, :, wide:].astype(BF16)

        return [
            send(sb[q].at[turn(dp, k, n_dp)], rb[q].at[k - 1], peer_dp(k)) for k in range(1, n_dp)
        ]

    def second_done(q, copies):
        for copy in copies:
            copy.wait_recv()
        total = acc[q][dp]
        for k in range(1, n_dp):
            total = total + rb[q][k - 1].astype(F32)
        high, wide = zb[q].shape[1:]
        for part in range(n_z):
            top = (part % row_parts) * high
            left = (part // row_parts) * wide
            value = total[top : top + high, left : left + wide]
            zf[q][part] = value
            zb[q][part] = value.astype(BF16)
        return [
            send(zb[q].at[turn(z, k, n_z)], rz[q].at[k - 1], peer_z(k)) for k in range(1, n_z)
        ]

    def third_done(q, copies):
        for copy in copies:
            copy.wait_recv()
        total = zf[q][z]
        for k in range(1, n_z):
            total = total + rz[q][k - 1].astype(F32)
        ag[q][core, z] = total.astype(BF16)
        own = ag[q].at[core, z]
        following = [send(own, own, peer_z(k)) for k in range(1, n_z)]
        shared = [send(own, own, sibling)]
        return following, shared

    def fourth_done(q, copies, shared):
        for k in range(1, n_z):
            copies[k - 1].wait_recv()
            got = ag[q].at[core, turn(z, -k, n_z)]
            shared.append(send(got, got, sibling))

    loads[2].wait()
    pair0 = other_half(0)
    pass_on(1, ds)
    own_half(0)
    step0 = pair_done(0, pair0)
    for copy in from_core[1]:
        copy.wait_recv()
    dhid[...] = dot(wd[:, :half], whole(ds, 0), 1, 1) + dot(wd[:, half:], whole(ds, 1), 1, 1)
    paired[...] = jnp.zeros(paired.shape, F32)

    @pl.loop(0, hid // strip)
    def backward(index):
        span = pl.ds(pl.multiple_of(index * strip, strip), strip)
        plain = dhid[span, :]
        paired[...] += jnp.sum(hidf[span, :] * plain, axis=0, keepdims=True)
        d_hidden = weight * plain
        turned[1][span, :] = (d_hidden * gate[span, :]).astype(BF16)
        turned[2][span, :] = (d_hidden * up[span, :]).astype(BF16)

    dg[...] = jnp.transpose(turned[1][...])
    du[...] = jnp.transpose(turned[2][...])
    share = paired[...]
    leading = share.astype(BF16).astype(F32)
    kept = jnp.where(named, leading, 0.0)
    rest = jnp.where(named, share - leading, 0.0)
    groups = [jnp.where(piece == k, kept, 0.0) for k in range(8)]
    groups += [jnp.where(piece == k, rest, 0.0) for k in range(8)]
    lanes = jnp.transpose(jnp.concatenate(groups, axis=0)).reshape(n_dp, rows, 128)
    wide = chunks[1][1]
    acc[1][:, :, wide : wide + 128] = lanes
    extra = acc[1].shape[2] - wide - 128
    if extra:
        acc[1][:, :, wide + 128 :] = jnp.zeros((n_dp, rows, extra), F32)

    pair1 = other_half(1)
    own_half(1)
    step1 = pair_done(1, pair1)
    pair2 = other_half(2)
    step0 = second_done(0, step0)
    own_half(2)
    step2 = pair_done(2, pair2)
    step1 = second_done(1, step1)
    keep(xs, xs_out)
    keep(ds, ds_out)
    for source, target in zip(turned, (hw_out, dg_out, du_out)):
        keep(source, target)
    step0, shared0 = third_done(0, step0)
    step2 = second_done(2, step2)
    step1, shared1 = third_done(1, step1)
    fourth_done(0, step0, shared0)
    step2, shared2 = third_done(2, step2)
    fourth_done(1, step1, shared1)
    fourth_done(2, step2, shared2)

    for q, (target, shared) in enumerate(
        ((mixed_out, shared0), (dtok_out, shared1), (dtok_out, shared2))
    ):
        for copy in shared:
            copy.wait_recv()
        first, width = chunks[q]
        high = zb[q].shape[1]
        for part in range(row_parts):
            span = slice(part * high, (part + 1) * high)
            routes = 0.0
            for side_core in range(CORES):
                strips = [ag[q][side_core, k * row_parts + part] for k in range(n_z // row_parts)]
                line = strips[0] if len(strips) == 1 else jnp.concatenate(strips, axis=1)
                left = side_core * half + first
                target[span, left : left + width] = line[:, :width]
                if q == 1:
                    routes = routes + line[:, width : width + 128].astype(F32)
            if q == 1:
                for by in (64, 32, 16, 8):
                    routes = routes + pltpu.roll(routes, by, 1)
                route_out[span, :] = routes
    for copy in sent:
        copy.wait_send()
    for copy in stores:
        copy.wait()


def finish(
    tile, route, mixed, d_tokens, xs, ds, hw, dg, du, route_out, mixed_out, dtok_out, gg, gu, gd,
    x_in, d_in, hw_in, dg_in, du_in, m_in, t_in, stage, load_sem, store_sem,
):
    def copy(source, target, sem):
        made = pltpu.make_async_copy(source, target, sem)
        made.start()
        return made

    moves = (
        (hw, hw_in), (ds, d_in), (mixed, m_in), (d_tokens, t_in), (dg, dg_in), (xs, x_in), (du, du_in)
    )
    loads = [copy(source, target, load_sem.at[k]) for k, (source, target) in enumerate(moves)]
    stores = []
    route_out[...] = jnp.transpose(route[...])[: route_out.shape[0]]
    half = xs.shape[3]
    total_rows = hw.shape[1]
    for number, (left, buffer, target, ready) in enumerate(
        ((hw_in, d_in, gd, 2), (dg_in, x_in, gg, 4), (du_in, x_in, gu, 1))
    ):
        for _ in range(ready):
            loads.pop(0).wait()
        if number == 1:
            stores.append(copy(m_in, mixed_out, store_sem.at[0]))
            stores.append(copy(t_in, dtok_out, store_sem.at[1]))
        for part in range(CORES):

            @pl.loop(0, half // tile)
            def columns(t):
                right = buffer[part, :, :, pl.ds(pl.multiple_of(t * tile, tile), tile)]
                start = pl.multiple_of(part * half + t * tile, tile)
                stage[number, :, pl.ds(start, tile)] = dot(
                    left[...], right.reshape(total_rows, tile), 1, 0
                ).astype(BF16)

            span = pl.ds(part * half, half)
            stores.append(
                copy(
                    stage.at[number, :, span], target.at[0, :, span],
                    store_sem.at[2 + CORES * number + part],
                )
            )
    for store in stores:
        store.wait()


def body(tokens, d_mixed, route_ids, route_weight, gate_weight, up_weight, down_weight):
    n_dp = lax.axis_size("dp")
    n_z = lax.axis_size("expert") // CORES
    rows, width = tokens.shape
    choices = route_ids.shape[1]
    hid = gate_weight.shape[1]
    half = width // CORES
    tile = 512
    row_parts = min(n_z, rows // 16)
    col_parts = n_z // row_parts
    high = rows // row_parts
    chunks = ((0, half), (0, half // 2), (half // 2, half // 2))
    plain_widths = tuple(wide for _, wide in chunks)
    widths = (half, half // 2 + 128 * col_parts, half // 2)
    total_rows = n_dp * rows

    def vmem(*dims, dtype=BF16):
        return pltpu.VMEM(dims, dtype)

    def each(make, sizes=widths):
        return [make(w) for w in sizes]

    scratch = [vmem(CORES, n_dp, rows, half)] * 2
    scratch += [vmem(hid, width)] * 3
    scratch += [vmem(hid, total_rows, dtype=F32)] * 4
    scratch += [vmem(8, total_rows, dtype=jnp.int32), vmem(8, total_rows, dtype=F32)]
    scratch += [vmem(1, total_rows, dtype=F32)]
    scratch += [vmem(hid, total_rows)] * 3
    scratch += [vmem(total_rows, hid)] * 3
    scratch += each(lambda w: vmem(n_dp, rows, w), plain_widths) * 2
    scratch += each(lambda w: vmem(n_dp, rows, w, dtype=F32))
    scratch += each(lambda w: vmem(n_dp, rows, w))
    scratch += each(lambda w: vmem(n_dp - 1, rows, w))
    scratch += each(lambda w: vmem(n_z, high, w // col_parts))
    scratch += each(lambda w: vmem(n_z, high, w // col_parts, dtype=F32))
    scratch += each(lambda w: vmem(n_z - 1, high, w // col_parts))
    scratch += each(lambda w: vmem(CORES, n_z, high, w // col_parts))
    gather = 4 * (n_dp - 1)
    reduce = len(chunks) * (n_dp + 3 * n_z - 2)
    copies = gather + reduce
    scratch += [pltpu.SemaphoreType.DMA((copies,))] * 2
    scratch += [pltpu.SemaphoreType.DMA((3,)), pltpu.SemaphoreType.DMA((5,))]

    in_vmem = pl.BlockSpec(memory_space=pltpu.VMEM)
    anywhere = pl.BlockSpec(memory_space=pl.ANY)
    flat = jax.ShapeDtypeStruct((rows, width), BF16)
    gathered = jax.ShapeDtypeStruct((CORES, n_dp, rows, half), BF16)
    left = jax.ShapeDtypeStruct((hid, total_rows), BF16)
    shape = (n_dp, n_z, rows, half, row_parts, tile, chunks)
    results = pl.pallas_call(
        functools.partial(kernel, shape),
        out_shape=(flat, jax.ShapeDtypeStruct((rows, 128), F32), flat)
        + (gathered,) * 2 + (left,) * 3,
        in_specs=[in_vmem] * 4 + [anywhere] * 3,
        out_specs=(in_vmem,) * 3 + (anywhere,) * 5,
        scratch_shapes=scratch,
        compiler_params=pltpu.CompilerParams(
            collective_id=0, has_side_effects=True, vmem_limit_bytes=60 * 1024 * 1024
        ),
        cost_estimate=pl.CostEstimate(
            flops=12 * total_rows * hid * width,
            bytes_accessed=6 * hid * width,
            transcendentals=total_rows * hid,
        ),
    )(tokens, d_mixed, route_ids.T, route_weight.T, gate_weight, up_weight, down_weight)

    mixed, route, d_tokens, *operands = results
    grad = jax.ShapeDtypeStruct((1, hid, width), BF16)
    route, mixed, d_tokens, grad_gate, grad_up, grad_down = pl.pallas_call(
        functools.partial(finish, 2 * tile),
        out_shape=(jax.ShapeDtypeStruct((choices, rows), F32), flat, flat, grad, grad, grad),
        in_specs=[in_vmem] + [anywhere] * 7,
        out_specs=(in_vmem,) + (anywhere,) * 5,
        scratch_shapes=[vmem(CORES, n_dp, rows, half)] * 2
        + [vmem(hid, total_rows)] * 3
        + [vmem(rows, width)] * 2
        + [vmem(3, hid, width), pltpu.SemaphoreType.DMA((7,)), pltpu.SemaphoreType.DMA((8,))],
        compiler_params=pltpu.CompilerParams(vmem_limit_bytes=60 * 1024 * 1024),
        cost_estimate=pl.CostEstimate(
            flops=6 * total_rows * hid * width,
            bytes_accessed=6 * hid * width,
            transcendentals=0,
        ),
    )(route, mixed, d_tokens, *operands)
    return mixed, route.T, d_tokens, grad_gate, grad_up, grad_down


def solution(mesh):
    row, whole, block = P("dp", None), P(), P(("expert", "dp"), None, None)
    return jax.shard_map(
        body,
        mesh=mesh,
        in_specs=(row, row, whole, whole, block, block, block),
        out_specs=(row, row, row, block, block, block),
        check_vma=False,
    )
```
